32 devices in a mesh: rep: 2 (over y), seq: 4 (over z), wt: 4 (over x, core).
Axes of the slice: x: 2, y: 2, z: 4, core: 2. Of those that a mesh axis runs over, the one named last changes fastest.
Arguments:
- tokens: bfloat16 [8, 16, 3072], P(('rep', 'wt'), 'seq'), parts along dimension 0, may hold values from -6 to 6
- modulation: float32 [8, 3, 3072], P(('rep', 'wt')), parts along dimension 0, may hold values from -3 to 3
- qkv_weight: bfloat16 [3072, 3, 3072], P('wt', None, 'seq'), may hold values from -0.109375 to 0.109375
- qkv_bias: float32 [3, 3072], P(None, 'seq'), may hold values from -3 to 3
- norm_gains: float32 [2, 128], replicated, may hold values from 0.1 to 1.9
- up_weight: bfloat16 [3072, 12288], P('wt', 'seq'), may hold values from -0.109375 to 0.109375
- up_mask: int32 [48, 192], P('wt', 'seq'), may hold values from 0 to 1, as said below
- up_bias: float32 [12288], P('seq'), may hold values from -3 to 3
- proj_weight: bfloat16 [3072, 3072], P('seq', 'wt'), may hold values from -0.109375 to 0.109375
- down_weight: bfloat16 [12288, 3072], P('seq', 'wt'), may hold values from -0.0546875 to 0.0546875
- down_mask: int32 [192, 48], P('seq', 'wt'), may hold values from 0 to 1, as said below
- out_bias: float32 [3072], replicated, may hold values from -3 to 3
Outputs:
- mixed: bfloat16 [8, 16, 3072], P(('rep', 'wt'), 'seq'), parts along dimension 0
The draws below stay inside these ranges and needn't reach their ends.
There are 2 independent parts, one for each index of `rep`. The reference program is written for one: setup_inputs(seed, part) draws one part's arguments, and reference() takes and returns one part's arrays. A program takes and returns all parts, laid end to end along the dimension named above; an argument that names none is the same for every part. Nothing has to cross between parts.
Inputs may be any that keep to these rules, and one draw needn't show every extreme that they name: `up_mask`: 1 keeps the 64 x 64 block of up_weight at that place, 0 drops it. `down_mask`: 1 keeps the 64 x 64 block of down_weight at that place, 0 drops it.
All inputs are finite; a program needn't handle non-finite values.
Results may differ from the reference program's by a relative error of at most 0.0039.
Values may be sent and summed in bfloat16 or wider, within the bound.
No kernel may reach another device: no remote copies, remote signals or barrier semaphores. Data moves between devices by JAX's collectives and lax.ppermute only.
A program may use at most 192 MiB of HBM per device.

```python
import math
import jax
import jax.numpy as jnp
from jax import lax

D = 3072
HEADS = 24
HEAD = 128
FF = 12288
BLOCK = 64
LEN = 16
IMAGES = 4


def keep_blocks(key, row_count, col_count):
    col_rate = jax.random.randint(jax.random.fold_in(key, 1), (1, col_count), 20, 95)
    row_shift = jax.random.randint(jax.random.fold_in(key, 2), (row_count, 1), -15, 6)
    tickets = jax.random.randint(jax.random.fold_in(key, 3), (row_count, col_count), 0, 100)
    return (tickets < col_rate + row_shift).astype(jnp.int32)


def draw_up_mask(key, part):
    key = jax.random.fold_in(key, 5)
    return keep_blocks(key, D // BLOCK, FF // BLOCK)


def draw_down_mask(key, part):
    key = jax.random.fold_in(key, 7)
    return keep_blocks(key, FF // BLOCK, D // BLOCK)


def level_of(own_key, dims, pieces, smallest, largest):
    loudness, own = 1.0, jax.random.fold_in(own_key, 6)
    for dim, shards_of in pieces:
        draws = jnp.exp(jax.random.uniform(jax.random.fold_in(own, dim), (shards_of,), jnp.float32, smallest / len(pieces), largest / len(pieces)))
        loudness = loudness * jnp.repeat(draws, dims[dim] // shards_of).reshape([-1 if axis == dim else 1 for axis in range(len(dims))])
    return loudness


def bell_draw(stream_key, extent, width, most, cuts=(), kind=jnp.bfloat16):
    entries = jax.random.normal(stream_key, extent, jnp.float32) * width
    if len(cuts) > 0:
        entries = level_of(stream_key, extent, cuts, -0.22, 0.18) * entries
    return jnp.clip(entries, min=-most, max=most).astype(kind)


def setup_inputs(seed: int = 0, part: int = 0) -> dict:
    keys = jax.random.split(jax.random.key(seed), 13)
    own_keys = jax.random.split(jax.random.fold_in(keys[12], part), 13)
    tokens = bell_draw(own_keys[0], (IMAGES, LEN, D), 1.0, 6.0, ((0, 4), (1, 4)))
    modulation = bell_draw(own_keys[1], (IMAGES, 3, D), 0.5, 3.0, ((0, 4),), jnp.float32)
    qkv_weight = bell_draw(keys[2], (D, 3, D), D ** -0.5, 0.109375, ((0, 4), (2, 4)))
    qkv_bias = bell_draw(keys[3], (3, D), 0.5, 3.0, ((1, 4),), jnp.float32)
    norm_gains = jnp.clip(1.0 + 0.18 * jax.random.normal(keys[4], (2, HEAD), jnp.float32), 0.1, 1.9)
    up_weight = bell_draw(keys[5], (D, FF), D ** -0.5, 0.109375, ((0, 4), (1, 4)))
    up_mask = draw_up_mask(jax.random.fold_in(keys[12], 71), part)
    up_bias = bell_draw(keys[7], (FF,), 0.5, 3.0, ((0, 4),), jnp.float32)
    proj_weight = bell_draw(keys[8], (D, D), D ** -0.5, 0.109375, ((0, 4), (1, 4)))
    down_weight = bell_draw(keys[9], (FF, D), FF ** -0.5, 0.0546875, ((0, 4), (1, 4)))
    down_mask = draw_down_mask(jax.random.fold_in(keys[12], 71), part)
    out_bias = bell_draw(keys[11], (D,), 0.5, 3.0, (), jnp.float32)
    return dict(tokens=tokens, modulation=modulation, qkv_weight=qkv_weight, qkv_bias=qkv_bias, norm_gains=norm_gains, up_weight=up_weight, up_mask=up_mask, up_bias=up_bias, proj_weight=proj_weight, down_weight=down_weight, down_mask=down_mask, out_bias=out_bias)


def expand_mask(keep_mask):
    expanded = jnp.repeat(jnp.repeat(keep_mask, BLOCK, axis=0), BLOCK, axis=1)
    return expanded.astype(jnp.bfloat16)

def layer_norm(values):
    center = values - lax.optimization_barrier(jnp.mean(values, axis=-1, keepdims=True))
    spread = lax.optimization_barrier(jnp.mean(center * center, axis=-1, keepdims=True))
    return center * lax.rsqrt(spread + 1e-06)

def rms_norm(values, gains):
    return values * lax.rsqrt(lax.optimization_barrier(jnp.mean(values * values, axis=-1, keepdims=True)) + 1e-06) * gains

def rounded(values):
    return lax.optimization_barrier(values.astype(jnp.bfloat16))

def reference(tokens, modulation, qkv_weight, qkv_bias, norm_gains, up_weight, up_mask, up_bias, proj_weight, down_weight, down_mask, out_bias):
    up_kept = up_weight * expand_mask(up_mask)
    down_kept = down_weight * expand_mask(down_mask)
    qkv_matrix = qkv_weight.reshape(D, 3 * D)

    def one_image(inputs):
        own_rows, mod_rows = inputs
        normed = layer_norm(own_rows.astype(jnp.float32))
        shaped = ((1.0 + mod_rows[1]) * normed + mod_rows[0]).astype(jnp.bfloat16)
        qkv_all = jnp.dot(shaped, qkv_matrix, preferred_element_type=jnp.float32).reshape(LEN, 3, D)
        qkv_all = (qkv_all + qkv_bias).astype(jnp.bfloat16)
        hidden = jax.nn.gelu(jnp.dot(shaped, up_kept, preferred_element_type=jnp.float32) + up_bias, approximate=True).astype(jnp.bfloat16)
        queries = rounded(rms_norm(qkv_all[:, 0].reshape(LEN, HEADS, HEAD).astype(jnp.float32), norm_gains[0]))
        keys_normed = rounded(rms_norm(qkv_all[:, 1].reshape(LEN, HEADS, HEAD).astype(jnp.float32), norm_gains[1]))
        values = qkv_all[:, 2].reshape(LEN, HEADS, HEAD)
        scores = jnp.einsum('qhd,khd->hqk', queries.astype(jnp.float32), keys_normed.astype(jnp.float32)) / math.sqrt(HEAD)
        weights = jnp.exp(scores)
        denoms = lax.optimization_barrier(jnp.sum(weights, axis=2))
        summed = jnp.einsum('hqk,khd->qhd', rounded(weights).astype(jnp.float32), values.astype(jnp.float32))
        attended = (summed / denoms.T[:, :, None]).reshape(LEN, D).astype(jnp.bfloat16)
        branch = jnp.dot(attended, proj_weight, preferred_element_type=jnp.float32) + jnp.dot(hidden, down_kept, preferred_element_type=jnp.float32) + out_bias
        return (own_rows.astype(jnp.float32) + mod_rows[2] * branch).astype(jnp.bfloat16)
    return lax.map(one_image, (tokens, modulation))
```

```python
import functools
import math

import jax
import jax.numpy as jnp
from jax import lax
from jax.experimental import pallas as pl
from jax.experimental.pallas import tpu as pltpu
from jax.sharding import PartitionSpec as P

HEAD = 128
BLOCK = 64
MIB = 1024 * 1024


def masked(weight, keep_mask):
    row_blocks, col_blocks = keep_mask.shape
    expanded = jnp.broadcast_to(keep_mask[:, None, :, None], (row_blocks, BLOCK, col_blocks, BLOCK))
    return weight * expanded.reshape(weight.shape).astype(jnp.bfloat16)


def layer_norm(values):
    center = values - jnp.mean(values, axis=-1, keepdims=True)
    spread = jnp.mean(center * center, axis=-1, keepdims=True)
    return center * lax.rsqrt(spread + 1e-06)


def norm_heads(flat_rows, gains):
    shaped_rows = flat_rows.reshape(flat_rows.shape[0], -1, HEAD).astype(jnp.float32)
    scaled = (
        shaped_rows
        * lax.rsqrt(jnp.mean(shaped_rows * shaped_rows, axis=-1, keepdims=True) + 1e-06)
        * gains
    )
    return scaled.astype(jnp.bfloat16)


def attend(queries, keys_normed, values):
    scores = jnp.einsum(
        "qhd,khd->hqk", queries, keys_normed, preferred_element_type=jnp.float32
    ) / math.sqrt(HEAD)
    weights = jnp.exp(scores)
    denoms = jnp.sum(weights, axis=2)
    summed = jnp.einsum(
        "hqk,khd->qhd", weights.astype(jnp.bfloat16), values, preferred_element_type=jnp.float32
    )
    return (summed, denoms)


def gathered_shards(
    tokens,
    modulation,
    qkv_weight,
    qkv_bias,
    norm_gains,
    up_weight,
    up_mask,
    up_bias,
    proj_weight,
    down_weight,
    down_mask,
    out_bias,
):
    own_rows = tokens[0]
    mod_rows = modulation[0]
    row_count = own_rows.shape[0]
    feature_count = own_rows.shape[1]
    head_count = feature_count // HEAD
    normed = layer_norm(own_rows.astype(jnp.float32))
    shaped = ((1.0 + mod_rows[1]) * normed + mod_rows[0]).astype(jnp.bfloat16)
    gathered = lax.all_gather(shaped, "seq", axis=0, tiled=True)
    seq_len = gathered.shape[0]
    col_share = qkv_weight.shape[2]
    up_local = masked(up_weight, up_mask)
    pieces = (
        lax.all_gather(qkv_weight, "wt", axis=0, tiled=True),
        lax.all_gather(up_local, "wt", axis=0, tiled=True),
    )
    piece_rows = pieces[0].shape[0]
    first = jnp.dot(
        gathered, pieces[0].reshape(piece_rows, 3 * col_share), preferred_element_type=jnp.float32
    )
    second = jnp.dot(gathered, pieces[1], preferred_element_type=jnp.float32)
    qkv_local = (first.reshape(seq_len, 3, col_share) + qkv_bias).astype(jnp.bfloat16)
    hidden = jax.nn.gelu(second + up_bias, approximate=True).astype(jnp.bfloat16)
    query_flat = lax.all_to_all(qkv_local[:, 0, :], "seq", split_axis=0, concat_axis=1, tiled=True)
    kv_whole = lax.all_gather(qkv_local[:, 1:, :], "seq", axis=2, tiled=True)
    queries = norm_heads(query_flat, norm_gains[0])
    keys_normed = norm_heads(kv_whole[:, 0, :], norm_gains[1])
    values = kv_whole[:, 1, :].reshape(seq_len, head_count, HEAD)
    summed, denoms = attend(queries, keys_normed, values)
    attended = (
        (summed / denoms.T[:, :, None]).reshape(row_count, feature_count).astype(jnp.bfloat16)
    )
    attended_cols = lax.all_to_all(attended, "seq", split_axis=1, concat_axis=0, tiled=True)
    down_local = masked(down_weight, down_mask)
    proj_full, down_full = (
        lax.all_gather(proj_weight, "wt", axis=1, tiled=True),
        lax.all_gather(down_local, "wt", axis=1, tiled=True),
    )
    branch_sum = lax.psum_scatter(
        jnp.dot(attended_cols, proj_full, preferred_element_type=jnp.float32)
        + jnp.dot(hidden, down_full, preferred_element_type=jnp.float32),
        "seq",
        scatter_dimension=0,
        tiled=True,
    )
    result = own_rows.astype(jnp.float32) + mod_rows[2] * (branch_sum + out_bias)
    return result.astype(jnp.bfloat16)[None]


def spread_lanes(mask, lanes):
    cols = mask.shape[1]
    pick = (
        lax.broadcasted_iota(jnp.int32, (cols, lanes), 1) // BLOCK
        == lax.broadcasted_iota(jnp.int32, (cols, lanes), 0)
    ).astype(jnp.bfloat16)
    return jnp.dot(mask.astype(jnp.bfloat16), pick, preferred_element_type=jnp.float32).astype(jnp.bfloat16)


def mask_rows(weight, spread):
    return jnp.concatenate(
        [weight[b * BLOCK : (b + 1) * BLOCK] * spread[b : b + 1] for b in range(spread.shape[0])], axis=0
    )


def in_kernel(qkv_steps, x_ref, wqkv_ref, up_ref, mask_ref, keep_ref, send_ref):
    i = pl.program_id(0)
    half = x_ref.shape[0] // 2

    def put(out):
        keep_ref[...] = out[:half]
        send_ref[...] = out[half:].astype(jnp.bfloat16)

    @pl.when(i < qkv_steps)
    def _():
        put(jnp.dot(x_ref[...], wqkv_ref[...], preferred_element_type=jnp.float32))

    @pl.when(i >= qkv_steps)
    def _():
        weight = mask_rows(up_ref[...], spread_lanes(mask_ref[...], up_ref.shape[1]))
        put(jnp.dot(x_ref[...], weight, preferred_element_type=jnp.float32))


def in_products(x, qkv_weight, up_weight, up_mask):
    rows, depth = x.shape
    share = qkv_weight.shape[2]
    hidden = up_weight.shape[1]
    ff_steps = hidden // share
    steps = 3 + ff_steps
    blocks = share // BLOCK
    masks = up_mask.reshape(-1, ff_steps, blocks).transpose(1, 0, 2)
    half = rows // 2
    return pl.pallas_call(
        functools.partial(in_kernel, 3),
        grid=(steps,),
        in_specs=[
            pl.BlockSpec((rows, depth), lambda i: (0, 0)),
            pl.BlockSpec((None, depth, share), lambda i: (jnp.minimum(i, 2), 0, 0)),
            pl.BlockSpec((depth, share), lambda i: (0, jnp.maximum(i - 3, 0))),
            pl.BlockSpec((None, depth // BLOCK, blocks), lambda i: (jnp.maximum(i - 3, 0), 0, 0)),
        ],
        out_specs=[
            pl.BlockSpec((half, share), lambda i: (0, i)),
            pl.BlockSpec((half, share), lambda i: (0, i)),
        ],
        out_shape=[
            jax.ShapeDtypeStruct((half, steps * share), jnp.float32),
            jax.ShapeDtypeStruct((half, steps * share), jnp.bfloat16),
        ],
        compiler_params=pltpu.CompilerParams(vmem_limit_bytes=40 * MIB),
        name="in_products",
    )(x, qkv_weight.transpose(1, 0, 2), up_weight, masks)


def mid_kernel(images, own_ref, other_ref, qkv_bias_ref, gains_ref, up_bias_ref, out_ref):
    rows = own_ref.shape[0]
    share = qkv_bias_ref.shape[1]
    heads = share // HEAD
    length = rows // images

    def total(start, size):
        return own_ref[:, start : start + size] + other_ref[:, start : start + size].astype(jnp.float32)

    def stacked(which):
        flat = (total(which * share, share) + qkv_bias_ref[which : which + 1, :]).astype(jnp.bfloat16)
        return jnp.concatenate([flat[:, h * HEAD : (h + 1) * HEAD] for h in range(heads)], axis=0)

    def normed(which):
        wide = stacked(which).astype(jnp.float32)
        scale = lax.rsqrt(jnp.mean(wide * wide, axis=-1, keepdims=True) + 1e-06)
        return (wide * scale * gains_ref[which : which + 1, :]).astype(jnp.bfloat16)

    queries, keys, values = normed(0), normed(1), stacked(2)
    scores = lax.dot_general(
        queries, keys, (((1,), (1,)), ((), ())), preferred_element_type=jnp.float32
    ) * (1.0 / math.sqrt(HEAD))
    size = heads * rows
    same = (
        lax.broadcasted_iota(jnp.int32, (size, size), 0) // length
        == lax.broadcasted_iota(jnp.int32, (size, size), 1) // length
    )
    weights = jnp.where(same, jnp.exp(jnp.where(same, scores, 0.0)), 0.0)
    denoms = jnp.sum(weights, axis=-1, keepdims=True)
    summed = jnp.dot(weights.astype(jnp.bfloat16), values, preferred_element_type=jnp.float32)
    attended = (summed / denoms).astype(jnp.bfloat16)
    for h in range(heads):
        out_ref[:, h * HEAD : (h + 1) * HEAD] = attended[h * rows : (h + 1) * rows]
    hidden = out_ref.shape[1] - share
    for start in range(0, hidden, share):
        v = total(3 * share + start, share) + up_bias_ref[:, start : start + share]
        cubic = math.sqrt(2.0 / math.pi) * (v + 0.044715 * (v * v * v))
        out_ref[:, share + start : 2 * share + start] = (0.5 * v * (1.0 + jnp.tanh(cubic))).astype(jnp.bfloat16)


def middle(images, own, other, qkv_bias, gains, up_bias):
    rows = own.shape[0]
    share = qkv_bias.shape[1]
    width = own.shape[1] - 2 * share
    return pl.pallas_call(
        functools.partial(mid_kernel, images),
        out_shape=jax.ShapeDtypeStruct((rows, width), jnp.bfloat16),
        compiler_params=pltpu.CompilerParams(vmem_limit_bytes=40 * MIB),
        name="middle",
    )(own, other, qkv_bias, gains, up_bias.reshape(1, -1))


def out_kernel(a_ref, b_ref, proj_ref, down_ref, mask_ref, out_ref, acc_ref):
    i = pl.program_id(0)
    x = jnp.concatenate([a_ref[...], b_ref[...]], axis=0)

    @pl.when(i == 0)
    def _():
        acc_ref[...] = jnp.dot(x, proj_ref[...], preferred_element_type=jnp.float32)

    @pl.when(i > 0)
    def _():
        weight = mask_rows(down_ref[...], spread_lanes(mask_ref[...], down_ref.shape[1]))
        acc_ref[...] += jnp.dot(x, weight, preferred_element_type=jnp.float32)

    @pl.when(i == pl.num_programs(0) - 1)
    def _():
        out_ref[...] = acc_ref[...].astype(jnp.bfloat16)


def out_products(mine, theirs, proj_weight, down_weight, down_mask):
    half = mine.shape[0]
    depth, width = proj_weight.shape
    steps = mine.shape[1] // depth
    blocks = depth // BLOCK
    masks = down_mask.reshape(steps - 1, blocks, -1)
    return pl.pallas_call(
        out_kernel,
        grid=(steps,),
        in_specs=[
            pl.BlockSpec((half, depth), lambda i: (0, i)),
            pl.BlockSpec((half, depth), lambda i: (0, i)),
            pl.BlockSpec((depth, width), lambda i: (0, 0)),
            pl.BlockSpec((depth, width), lambda i: (jnp.maximum(i - 1, 0), 0)),
            pl.BlockSpec((None, blocks, width // BLOCK), lambda i: (jnp.maximum(i - 1, 0), 0, 0)),
        ],
        out_specs=pl.BlockSpec((2 * half, width), lambda i: (0, 0)),
        out_shape=jax.ShapeDtypeStruct((2 * half, width), jnp.bfloat16),
        scratch_shapes=[pltpu.VMEM((2 * half, width), jnp.float32)],
        compiler_params=pltpu.CompilerParams(vmem_limit_bytes=40 * MIB),
        name="out_products",
    )(mine, theirs, proj_weight, down_weight, masks)


def swap(values, bit):
    count = lax.axis_size("wt")
    return lax.ppermute(values, "wt", [(i, i ^ bit) for i in range(count)])


def fixed_shards(
    tokens,
    modulation,
    qkv_weight,
    qkv_bias,
    norm_gains,
    up_weight,
    up_mask,
    up_bias,
    proj_weight,
    down_weight,
    down_mask,
    out_bias,
):
    both = ("seq", "wt")
    seq, wt = lax.axis_size("seq"), lax.axis_size("wt")
    me = lax.axis_index("wt")
    own_rows = tokens[0]
    mod_rows = modulation[0]
    count, features = own_rows.shape
    share = features // wt
    normed = layer_norm(own_rows.astype(jnp.float32))
    shaped = ((1.0 + mod_rows[1]) * normed + mod_rows[0]).astype(jnp.bfloat16)
    sent = jnp.broadcast_to(shaped.reshape(count, wt, share).transpose(1, 0, 2)[None], (seq, wt, count, share))
    got = lax.all_to_all(sent.reshape(seq * wt, count, share), both, split_axis=0, concat_axis=0, tiled=True)
    got = got.reshape(seq, wt, count, share)
    rows = jnp.concatenate(
        [
            lax.dynamic_index_in_dim(got, me ^ j, 1, keepdims=False).reshape(seq * count, share)
            for j in (0, 2, 1, 3)
        ],
        axis=0,
    )
    kept, given = in_products(rows, qkv_weight, up_weight, up_mask)
    pair = kept + swap(given, 1).astype(jnp.float32)
    length = seq * count
    turned = jnp.concatenate([pair[length:], pair[:length]], axis=0).astype(jnp.bfloat16)
    mixed = middle(2, pair, swap(turned, 2), qkv_bias, norm_gains, up_bias)
    shares = out_products(mixed, swap(mixed, 1), proj_weight, down_weight, down_mask)
    shares = shares.reshape(wt, seq, count, share)
    order = (0, 2, 1, 3)
    place = jnp.array([order.index(j) for j in range(wt)], jnp.int32)
    home = jnp.stack(
        [lax.dynamic_index_in_dim(shares, place[me ^ i], 0, keepdims=False) for i in range(wt)], axis=1
    )
    back = lax.all_to_all(home.reshape(seq * wt, count, share), both, split_axis=0, concat_axis=0, tiled=True)
    branch = jnp.sum(back.reshape(seq, wt, count, share).astype(jnp.float32), axis=0)
    branch = branch.transpose(1, 0, 2).reshape(count, features)
    result = own_rows.astype(jnp.float32) + mod_rows[2] * (branch + out_bias)
    return result.astype(jnp.bfloat16)[None]


def solution(mesh):
    seq, wt = mesh.shape["seq"], mesh.shape["wt"]

    def shards(*args):
        share = args[2].shape[2]
        whole_heads = share % HEAD == 0 and share == args[8].shape[1] and args[5].shape[1] % share == 0
        fits = whole_heads and wt == 4 and (seq * args[0].shape[1]) % 16 == 0
        return (fixed_shards if fits else gathered_shards)(*args)

    return jax.shard_map(
        shards,
        mesh=mesh,
        in_specs=(
            P(("rep", "wt"), "seq", None),
            P(("rep", "wt"), None, None),
            P("wt", None, "seq"),
            P(None, "seq"),
            P(),
            P("wt", "seq"),
            P("wt", "seq"),
            P("seq"),
            P("seq", "wt"),
            P("seq", "wt"),
            P("seq", "wt"),
            P(),
        ),
        out_specs=P(("rep", "wt"), "seq", None),
        check_vma=False,
    )
```

```python
import functools
import math

import jax
import jax.numpy as jnp
from jax import lax
from jax.experimental import pallas as pl
from jax.experimental.pallas import tpu as pltpu
from jax.sharding import PartitionSpec as P

HEAD = 128
BLOCK = 64
MIB = 1024 * 1024
ENTER = 50
BESIDE = 16 * MIB


def masked(weight, keep_mask):
    row_blocks, col_blocks = keep_mask.shape
    expanded = jnp.broadcast_to(keep_mask[:, None, :, None], (row_blocks, BLOCK, col_blocks, BLOCK))
    return weight * expanded.reshape(weight.shape).astype(jnp.bfloat16)


def layer_norm(values):
    center = values - jnp.mean(values, axis=-1, keepdims=True)
    spread = jnp.mean(center * center, axis=-1, keepdims=True)
    return center * lax.rsqrt(spread + 1e-06)


def norm_heads(flat_rows, gains):
    shaped_rows = flat_rows.reshape(flat_rows.shape[0], -1, HEAD).astype(jnp.float32)
    scaled = (
        shaped_rows
        * lax.rsqrt(jnp.mean(shaped_rows * shaped_rows, axis=-1, keepdims=True) + 1e-06)
        * gains
    )
    return scaled.astype(jnp.bfloat16)


def attend(queries, keys_normed, values):
    scores = jnp.einsum(
        "qhd,khd->hqk", queries, keys_normed, preferred_element_type=jnp.float32
    ) / math.sqrt(HEAD)
    weights = jnp.exp(scores)
    denoms = jnp.sum(weights, axis=2)
    summed = jnp.einsum(
        "hqk,khd->qhd", weights.astype(jnp.bfloat16), values, preferred_element_type=jnp.float32
    )
    return (summed, denoms)


def gathered_shards(
    tokens,
    modulation,
    qkv_weight,
    qkv_bias,
    norm_gains,
    up_weight,
    up_mask,
    up_bias,
    proj_weight,
    down_weight,
    down_mask,
    out_bias,
):
    own_rows = tokens[0]
    mod_rows = modulation[0]
    row_count = own_rows.shape[0]
    feature_count = own_rows.shape[1]
    head_count = feature_count // HEAD
    normed = layer_norm(own_rows.astype(jnp.float32))
    shaped = ((1.0 + mod_rows[1]) * normed + mod_rows[0]).astype(jnp.bfloat16)
    gathered = lax.all_gather(shaped, "seq", axis=0, tiled=True)
    seq_len = gathered.shape[0]
    col_share = qkv_weight.shape[2]
    up_local = masked(up_weight, up_mask)
    pieces = (
        lax.all_gather(qkv_weight, "wt", axis=0, tiled=True),
        lax.all_gather(up_local, "wt", axis=0, tiled=True),
    )
    piece_rows = pieces[0].shape[0]
    first = jnp.dot(
        gathered, pieces[0].reshape(piece_rows, 3 * col_share), preferred_element_type=jnp.float32
    )
    second = jnp.dot(gathered, pieces[1], preferred_element_type=jnp.float32)
    qkv_local = (first.reshape(seq_len, 3, col_share) + qkv_bias).astype(jnp.bfloat16)
    hidden = jax.nn.gelu(second + up_bias, approximate=True).astype(jnp.bfloat16)
    query_flat = lax.all_to_all(qkv_local[:, 0, :], "seq", split_axis=0, concat_axis=1, tiled=True)
    kv_whole = lax.all_gather(qkv_local[:, 1:, :], "seq", axis=2, tiled=True)
    queries = norm_heads(query_flat, norm_gains[0])
    keys_normed = norm_heads(kv_whole[:, 0, :], norm_gains[1])
    values = kv_whole[:, 1, :].reshape(seq_len, head_count, HEAD)
    summed, denoms = attend(queries, keys_normed, values)
    attended = (
        (summed / denoms.T[:, :, None]).reshape(row_count, feature_count).astype(jnp.bfloat16)
    )
    attended_cols = lax.all_to_all(attended, "seq", split_axis=1, concat_axis=0, tiled=True)
    down_local = masked(down_weight, down_mask)
    proj_full, down_full = (
        lax.all_gather(proj_weight, "wt", axis=1, tiled=True),
        lax.all_gather(down_local, "wt", axis=1, tiled=True),
    )
    branch_sum = lax.psum_scatter(
        jnp.dot(attended_cols, proj_full, preferred_element_type=jnp.float32)
        + jnp.dot(hidden, down_full, preferred_element_type=jnp.float32),
        "seq",
        scatter_dimension=0,
        tiled=True,
    )
    result = own_rows.astype(jnp.float32) + mod_rows[2] * (branch_sum + out_bias)
    return result.astype(jnp.bfloat16)[None]


def enter_kernel(tokens_hbm, mod_hbm, keep_ref, send_ref, tokens_ref, mod_ref, sems):
    copies = [
        pltpu.make_async_copy(tokens_hbm, tokens_ref, sems.at[0]),
        pltpu.make_async_copy(mod_hbm, mod_ref, sems.at[1]),
    ]
    for copy in copies:
        copy.start()
    for copy in copies:
        copy.wait()
    rows = tokens_ref[0].astype(jnp.float32)
    shaped = ((1.0 + mod_ref[1]) * layer_norm(rows) + mod_ref[0]).astype(jnp.bfloat16)
    share = keep_ref.shape[1] // 2
    even = lax.axis_index("wt") % 2 == 0
    for x in range(2):
        first = shaped[:, 2 * x * share : (2 * x + 1) * share]
        second = shaped[:, (2 * x + 1) * share : (2 * x + 2) * share]
        keep_ref[:, x * share : (x + 1) * share] = jnp.where(even, first, second)
        send_ref[:, x * share : (x + 1) * share] = jnp.where(even, second, first)


def enter(tokens, modulation):
    _, count, features = tokens.shape
    turned = modulation.transpose(1, 0, 2)
    return pl.pallas_call(
        enter_kernel,
        in_specs=[pl.BlockSpec(memory_space=pltpu.HBM)] * 2,
        out_shape=[jax.ShapeDtypeStruct((count, features // 2), jnp.bfloat16)] * 2,
        scratch_shapes=[
            pltpu.VMEM(tokens.shape, tokens.dtype),
            pltpu.VMEM(turned.shape, turned.dtype),
            pltpu.SemaphoreType.DMA((2,)),
        ],
        compiler_params=pltpu.CompilerParams(vmem_limit_bytes=ENTER * MIB),
        cost_estimate=pl.CostEstimate(flops=0, bytes_accessed=0, transcendentals=0),
        name="enter",
    )(tokens, turned)


def quarters(ref, start, count):
    return ref[start : start + count].astype(jnp.float32)


def on_first():
    return lax.axis_index("wt") < 2


def apart(kept, got, mine_ref, send_ref):
    first = jnp.concatenate([kept[0], got[0]], axis=0)
    second = jnp.concatenate([kept[1], got[1]], axis=0)
    mine_ref[...] = jnp.where(on_first(), first, second).astype(mine_ref.dtype)
    send_ref[...] = jnp.where(on_first(), second, first).astype(send_ref.dtype)


def part_kernel(kept_ref, got_ref, mine_ref, send_ref):
    share = mine_ref.shape[1]
    halves = [[ref[:, :share].astype(jnp.float32), ref[:, share:].astype(jnp.float32)] for ref in (kept_ref, got_ref)]
    apart(*halves, mine_ref, send_ref)


def near_kernel(mine_ref, theirs_ref, out_ref):
    count = mine_ref.shape[0] // 2
    pieces = []
    for start in (0, count):
        mine, theirs = quarters(mine_ref, start, count), quarters(theirs_ref, start, count)
        pieces += [jnp.where(on_first(), mine, theirs), jnp.where(on_first(), theirs, mine)]
    out_ref[...] = jnp.concatenate(pieces, axis=0).astype(out_ref.dtype)


def fold_kernel(kept_ref, got_ref, keep_ref, send_ref):
    size = keep_ref.shape[0] // 2
    total = kept_ref[...] + got_ref[...].astype(jnp.float32)
    keep_ref[...] = jnp.concatenate([total[:size], total[2 * size : 3 * size]], axis=0)
    send_ref[...] = jnp.concatenate([total[size : 2 * size], total[3 * size :]], axis=0).astype(send_ref.dtype)


def divide_kernel(kept_ref, got_ref, mine_ref, send_ref):
    count = mine_ref.shape[0] // 2
    total = kept_ref[...] + got_ref[...].astype(jnp.float32)
    rows = [total[n * count : (n + 1) * count] for n in range(4)]
    apart(rows[:2], rows[2:], mine_ref, send_ref)


def join_kernel(mine_ref, theirs_ref, here_ref, send_ref):
    count = mine_ref.shape[0] // 2
    for start, ref in ((0, here_ref), (count, send_ref)):
        mine, theirs = quarters(mine_ref, start, count), quarters(theirs_ref, start, count)
        ref[...] = jnp.concatenate(
            [jnp.where(on_first(), mine, theirs), jnp.where(on_first(), theirs, mine)], axis=0
        )


def leave_kernel(here_ref, there_ref, tokens_ref, mod_ref, bias_ref, out_ref):
    count, share = here_ref.shape[0] // 2, here_ref.shape[1]
    even = lax.axis_index("wt") % 2 == 0
    for n in range(4):
        lanes = slice(n * share, (n + 1) * share)
        here, there = quarters(here_ref, n // 2 * count, count), quarters(there_ref, n // 2 * count, count)
        branch = jnp.where(even == (n % 2 == 0), here, there) + bias_ref[:, lanes]
        out_ref[0, :, lanes] = (tokens_ref[0, :, lanes].astype(jnp.float32) + mod_ref[2, :, lanes] * branch).astype(out_ref.dtype)


def small(kernel, outs, *args, beside=0):
    return pl.pallas_call(
        kernel,
        out_shape=outs,
        compiler_params=pltpu.CompilerParams(vmem_limit_bytes=4 * MIB),
        cost_estimate=pl.CostEstimate(flops=400 * beside, bytes_accessed=beside, transcendentals=beside // 100) if beside else None,
        name=kernel.__name__,
    )(*args)


def pick_lanes(blocks, lanes):
    return (
        lax.broadcasted_iota(jnp.int32, (blocks, lanes), 1) // BLOCK
        == lax.broadcasted_iota(jnp.int32, (blocks, lanes), 0)
    ).astype(jnp.bfloat16)


def prune_kernel(mask_dim, mask_ref, weight_ref, out_ref, lanes):
    lanes[...] = lax.dot_general(
        mask_ref[...].astype(jnp.bfloat16),
        pick_lanes(mask_ref.shape[mask_dim], out_ref.shape[1]),
        (((mask_dim,), (0,)), ((), ())),
        preferred_element_type=jnp.float32,
    )

    def body(b, _):
        rows = pl.ds(pl.multiple_of(b * BLOCK, BLOCK), BLOCK)
        out_ref[rows, :] = weight_ref[rows, :] * lanes[pl.ds(b, 1), :].astype(jnp.bfloat16)
        return 0

    lax.fori_loop(0, out_ref.shape[0] // BLOCK, body, 0)


def prune(weight, mask, turned):
    size = 2 * weight.size
    return pl.pallas_call(
        functools.partial(prune_kernel, 0 if turned else 1),
        out_shape=jax.ShapeDtypeStruct(weight.shape, jnp.bfloat16),
        scratch_shapes=[pltpu.VMEM((weight.shape[0] // BLOCK, weight.shape[1]), jnp.float32)],
        compiler_params=pltpu.CompilerParams(vmem_limit_bytes=14 * MIB),
        cost_estimate=pl.CostEstimate(flops=size, bytes_accessed=2 * size, transcendentals=0),
        name="prune",
    )(mask.T if turned else mask, weight)


def in_kernel(share, a_ref, b_ref, w_ref, keep_ref, send_ref):
    x = jnp.concatenate([a_ref[...], b_ref[...]], axis=0)
    rows = x.shape[0]
    for n in range(keep_ref.shape[1] // share):
        lanes = slice(n * share, (n + 1) * share)
        weight = w_ref[n] if len(w_ref.shape) == 3 else w_ref[:, lanes]
        out = jnp.dot(x, weight, preferred_element_type=jnp.float32)
        keep_ref[:, lanes] = jnp.concatenate([out[r : r + 8] for r in range(0, rows, 16)], axis=0)
        send_ref[:, lanes] = jnp.concatenate([out[r + 8 : r + 16] for r in range(0, rows, 16)], axis=0).astype(jnp.bfloat16)


def in_products(near, far, weight):
    half, depth = near.shape
    rows = 2 * half
    width = weight.size // depth
    return pl.pallas_call(
        functools.partial(in_kernel, depth),
        out_shape=[
            jax.ShapeDtypeStruct((half, width), jnp.float32),
            jax.ShapeDtypeStruct((half, width), jnp.bfloat16),
        ],
        compiler_params=pltpu.CompilerParams(vmem_limit_bytes=12 * MIB),
        cost_estimate=pl.CostEstimate(
            flops=2 * rows * weight.size, bytes_accessed=2 * weight.size, transcendentals=0
        ),
        name="in_products",
    )(near, far, weight)


def attend_kernel(images, part, own_ref, other_ref, bias_ref, gains_ref, out_ref):
    rows, share = out_ref.shape
    heads = share // HEAD

    def stacked(which):
        lanes = slice(which * share, (which + 1) * share)
        flat = own_ref[:, lanes] + other_ref[:, lanes].astype(jnp.float32)
        flat = (flat + bias_ref[which : which + 1, :]).astype(jnp.bfloat16)
        return jnp.concatenate([flat[:, h * HEAD : (h + 1) * HEAD] for h in range(heads)], axis=0)

    def normed(which):
        wide = stacked(which).astype(jnp.float32)
        scale = lax.rsqrt(jnp.mean(wide * wide, axis=-1, keepdims=True) + 1e-06)
        return (wide * scale * gains_ref[which : which + 1, :]).astype(jnp.bfloat16)

    queries, keys, values = normed(0), normed(1), stacked(2)
    scores = lax.dot_general(
        queries, keys, (((1,), (1,)), ((), ())), preferred_element_type=jnp.float32
    ) * (1.0 / math.sqrt(HEAD))
    size = heads * rows

    def group(dim):
        place = lax.broadcasted_iota(jnp.int32, (size, size), dim)
        return place // rows * images + place // part % images

    same = group(0) == group(1)
    weights = jnp.where(same, jnp.exp(jnp.where(same, scores, 0.0)), 0.0)
    denoms = jnp.sum(weights, axis=-1, keepdims=True)
    summed = jnp.dot(weights.astype(jnp.bfloat16), values, preferred_element_type=jnp.float32)
    attended = (summed / denoms).astype(jnp.bfloat16)
    for h in range(heads):
        out_ref[:, h * HEAD : (h + 1) * HEAD] = attended[h * rows : (h + 1) * rows]


def attention(images, part, own, other, bias, gains):
    return pl.pallas_call(
        functools.partial(attend_kernel, images, part),
        out_shape=jax.ShapeDtypeStruct((own.shape[0], bias.shape[1]), jnp.bfloat16),
        compiler_params=pltpu.CompilerParams(vmem_limit_bytes=8 * MIB),
        name="attention",
    )(own, other, bias, gains)


def hidden_kernel(own_ref, other_ref, bias_ref, out_ref):
    step = 6 * HEAD
    for start in range(0, out_ref.shape[1], step):
        lanes = slice(start, start + step)
        v = own_ref[:, lanes] + other_ref[:, lanes].astype(jnp.float32) + bias_ref[:, lanes]
        cubic = math.sqrt(2.0 / math.pi) * (v + 0.044715 * (v * v * v))
        out_ref[:, lanes] = (0.5 * v * (1.0 + jnp.tanh(cubic))).astype(jnp.bfloat16)


def activate(own, other, bias):
    return pl.pallas_call(
        hidden_kernel,
        out_shape=jax.ShapeDtypeStruct(own.shape, jnp.bfloat16),
        compiler_params=pltpu.CompilerParams(vmem_limit_bytes=8 * MIB),
        name="hidden",
    )(own, other, bias.reshape(1, -1))


def out_kernel(a_mine, a_theirs, h_mine, h_theirs, proj_ref, down_ref, keep_ref, send_ref):
    attended = jnp.concatenate([a_mine[...], a_theirs[...]], axis=0)
    hidden = jnp.concatenate([h_mine[...], h_theirs[...]], axis=0)
    total = jnp.dot(attended, proj_ref[...], preferred_element_type=jnp.float32)
    total += jnp.dot(hidden, down_ref[...], preferred_element_type=jnp.float32)
    part = total.shape[0] // 4
    keep_ref[...] = jnp.concatenate([total[:part], total[2 * part : 3 * part]], axis=0)
    send_ref[...] = jnp.concatenate([total[part : 2 * part], total[3 * part :]], axis=0).astype(jnp.bfloat16)


def out_products(mine, theirs, hidden, hidden_theirs, proj, down):
    half, width = mine.shape[0], proj.shape[1]
    size = proj.size + down.size
    return pl.pallas_call(
        out_kernel,
        out_shape=[
            jax.ShapeDtypeStruct((half, width), jnp.float32),
            jax.ShapeDtypeStruct((half, width), jnp.bfloat16),
        ],
        compiler_params=pltpu.CompilerParams(vmem_limit_bytes=12 * MIB),
        cost_estimate=pl.CostEstimate(flops=4 * half * size, bytes_accessed=2 * size, transcendentals=0),
        name="out_products",
    )(mine, theirs, hidden, hidden_theirs, proj, down)


def swap(values, axis, bit):
    count = lax.axis_size(axis)
    return lax.ppermute(values, axis, [(i, i ^ bit) for i in range(count)])


def fixed_shards(
    tokens,
    modulation,
    qkv_weight,
    qkv_bias,
    norm_gains,
    up_weight,
    up_mask,
    up_bias,
    proj_weight,
    down_weight,
    down_mask,
    out_bias,
):
    count, features = tokens.shape[1:]
    share = features // 4
    bf16, f32 = jnp.bfloat16, jnp.float32

    def rows_of(n, kind):
        return jax.ShapeDtypeStruct((n * count, share), kind)

    kept, given = enter(tokens, modulation)
    mine, given = small(part_kernel, [rows_of(2, bf16)] * 2, kept, swap(given, "wt", 1), beside=BESIDE)
    near = small(near_kernel, rows_of(4, bf16), mine, swap(given, "wt", 2), beside=BESIDE)
    up_pruned = prune(up_weight, up_mask, False)
    near, up_pruned = lax.optimization_barrier((near, up_pruned))
    near = jnp.concatenate([near, swap(near, "seq", 2)], axis=0)
    far = swap(near, "seq", 1)

    kept, given = in_products(near, far, qkv_weight.transpose(1, 0, 2))
    near, given = lax.optimization_barrier((near, given))
    up_kept, up_given = in_products(near, far, up_pruned)

    def reduced(kept, given):
        total = kept + swap(given, "wt", 1).astype(jnp.float32)
        return total, swap(total.astype(jnp.bfloat16), "wt", 2)

    qkv_pair, up_pair = reduced(kept, given), reduced(up_kept, up_given)
    down_pruned = prune(down_weight, down_mask, True)
    qkv_pair, up_pair, down_pruned = lax.optimization_barrier((qkv_pair, up_pair, down_pruned))
    attended = attention(2, count, *qkv_pair, qkv_bias, norm_gains)
    hidden = activate(*up_pair, up_bias)
    kept, given = out_products(
        attended, swap(attended, "wt", 1), hidden, swap(hidden, "wt", 1), proj_weight, down_pruned
    )
    kept, given = small(fold_kernel, [rows_of(4, f32), rows_of(4, bf16)], kept, swap(given, "seq", 1))
    mine, given = small(divide_kernel, [rows_of(2, f32)] * 2, kept, swap(given, "seq", 2))
    here, given = small(join_kernel, [rows_of(2, f32)] * 2, mine, swap(given, "wt", 2))
    there = swap(given, "wt", 1)
    out = jax.ShapeDtypeStruct(tokens.shape, tokens.dtype)
    return small(leave_kernel, out, here, there, tokens, modulation.transpose(1, 0, 2), out_bias.reshape(1, -1))


def solution(mesh):
    seq, wt = mesh.shape["seq"], mesh.shape["wt"]

    def shards(*args):
        share = args[2].shape[2]
        whole_heads = share % HEAD == 0 and share == args[8].shape[1] and args[5].shape[1] % share == 0
        fits = whole_heads and wt == 4 and seq == 4 and args[0].shape[1] == 4
        return (fixed_shards if fits else gathered_shards)(*args)

    return jax.shard_map(
        shards,
        mesh=mesh,
        in_specs=(
            P(("rep", "wt"), "seq", None),
            P(("rep", "wt"), None, None),
            P("wt", None, "seq"),
            P(None, "seq"),
            P(),
            P("wt", "seq"),
            P("wt", "seq"),
            P("seq"),
            P("seq", "wt"),
            P("seq", "wt"),
            P("seq", "wt"),
            P(),
        ),
        out_specs=P(("rep", "wt"), "seq", None),
        check_vma=False,
    )
```

```python
import functools
import math

import jax
import jax.numpy as jnp
from jax import lax
from jax.experimental import pallas as pl
from jax.experimental.pallas import tpu as pltpu
from jax.sharding import PartitionSpec as P

HEAD = 128
BLOCK = 64
MIB = 1024 * 1024
ENTER = 50
NEAR_FIRST = (0, 2, 1, 3)
BESIDE = 16 * MIB


def masked(weight, keep_mask):
    row_blocks, col_blocks = keep_mask.shape
    expanded = jnp.broadcast_to(keep_mask[:, None, :, None], (row_blocks, BLOCK, col_blocks, BLOCK))
    return weight * expanded.reshape(weight.shape).astype(jnp.bfloat16)


def layer_norm(values):
    center = values - jnp.mean(values, axis=-1, keepdims=True)
    spread = jnp.mean(center * center, axis=-1, keepdims=True)
    return center * lax.rsqrt(spread + 1e-06)


def norm_heads(flat_rows, gains):
    shaped_rows = flat_rows.reshape(flat_rows.shape[0], -1, HEAD).astype(jnp.float32)
    scaled = (
        shaped_rows
        * lax.rsqrt(jnp.mean(shaped_rows * shaped_rows, axis=-1, keepdims=True) + 1e-06)
        * gains
    )
    return scaled.astype(jnp.bfloat16)


def attend(queries, keys_normed, values):
    scores = jnp.einsum(
        "qhd,khd->hqk", queries, keys_normed, preferred_element_type=jnp.float32
    ) / math.sqrt(HEAD)
    weights = jnp.exp(scores)
    denoms = jnp.sum(weights, axis=2)
    summed = jnp.einsum(
        "hqk,khd->qhd", weights.astype(jnp.bfloat16), values, preferred_element_type=jnp.float32
    )
    return (summed, denoms)


def gathered_shards(
    tokens,
    modulation,
    qkv_weight,
    qkv_bias,
    norm_gains,
    up_weight,
    up_mask,
    up_bias,
    proj_weight,
    down_weight,
    down_mask,
    out_bias,
):
    own_rows = tokens[0]
    mod_rows = modulation[0]
    row_count = own_rows.shape[0]
    feature_count = own_rows.shape[1]
    head_count = feature_count // HEAD
    normed = layer_norm(own_rows.astype(jnp.float32))
    shaped = ((1.0 + mod_rows[1]) * normed + mod_rows[0]).astype(jnp.bfloat16)
    gathered = lax.all_gather(shaped, "seq", axis=0, tiled=True)
    seq_len = gathered.shape[0]
    col_share = qkv_weight.shape[2]
    up_local = masked(up_weight, up_mask)
    pieces = (
        lax.all_gather(qkv_weight, "wt", axis=0, tiled=True),
        lax.all_gather(up_local, "wt", axis=0, tiled=True),
    )
    piece_rows = pieces[0].shape[0]
    first = jnp.dot(
        gathered, pieces[0].reshape(piece_rows, 3 * col_share), preferred_element_type=jnp.float32
    )
    second = jnp.dot(gathered, pieces[1], preferred_element_type=jnp.float32)
    qkv_local = (first.reshape(seq_len, 3, col_share) + qkv_bias).astype(jnp.bfloat16)
    hidden = jax.nn.gelu(second + up_bias, approximate=True).astype(jnp.bfloat16)
    query_flat = lax.all_to_all(qkv_local[:, 0, :], "seq", split_axis=0, concat_axis=1, tiled=True)
    kv_whole = lax.all_gather(qkv_local[:, 1:, :], "seq", axis=2, tiled=True)
    queries = norm_heads(query_flat, norm_gains[0])
    keys_normed = norm_heads(kv_whole[:, 0, :], norm_gains[1])
    values = kv_whole[:, 1, :].reshape(seq_len, head_count, HEAD)
    summed, denoms = attend(queries, keys_normed, values)
    attended = (
        (summed / denoms.T[:, :, None]).reshape(row_count, feature_count).astype(jnp.bfloat16)
    )
    attended_cols = lax.all_to_all(attended, "seq", split_axis=1, concat_axis=0, tiled=True)
    down_local = masked(down_weight, down_mask)
    proj_full, down_full = (
        lax.all_gather(proj_weight, "wt", axis=1, tiled=True),
        lax.all_gather(down_local, "wt", axis=1, tiled=True),
    )
    branch_sum = lax.psum_scatter(
        jnp.dot(attended_cols, proj_full, preferred_element_type=jnp.float32)
        + jnp.dot(hidden, down_full, preferred_element_type=jnp.float32),
        "seq",
        scatter_dimension=0,
        tiled=True,
    )
    result = own_rows.astype(jnp.float32) + mod_rows[2] * (branch_sum + out_bias)
    return result.astype(jnp.bfloat16)[None]


def enter_kernel(tokens_hbm, mod_hbm, keep_ref, send_ref, tokens_ref, mod_ref, sems):
    copies = [
        pltpu.make_async_copy(tokens_hbm, tokens_ref, sems.at[0]),
        pltpu.make_async_copy(mod_hbm, mod_ref, sems.at[1]),
    ]
    for copy in copies:
        copy.start()
    for copy in copies:
        copy.wait()
    rows = tokens_ref[0].astype(jnp.float32)
    shaped = ((1.0 + mod_ref[1]) * layer_norm(rows) + mod_ref[0]).astype(jnp.bfloat16)
    share = keep_ref.shape[1] // 2
    even = lax.axis_index("wt") % 2 == 0
    for x in range(2):
        first = shaped[:, 2 * x * share : (2 * x + 1) * share]
        second = shaped[:, (2 * x + 1) * share : (2 * x + 2) * share]
        keep_ref[:, x * share : (x + 1) * share] = jnp.where(even, first, second)
        send_ref[:, x * share : (x + 1) * share] = jnp.where(even, second, first)


def enter(tokens, modulation):
    _, count, features = tokens.shape
    turned = modulation.transpose(1, 0, 2)
    return pl.pallas_call(
        enter_kernel,
        in_specs=[pl.BlockSpec(memory_space=pltpu.HBM)] * 2,
        out_shape=[jax.ShapeDtypeStruct((count, features // 2), jnp.bfloat16)] * 2,
        scratch_shapes=[
            pltpu.VMEM(tokens.shape, tokens.dtype),
            pltpu.VMEM(turned.shape, turned.dtype),
            pltpu.SemaphoreType.DMA((2,)),
        ],
        compiler_params=pltpu.CompilerParams(vmem_limit_bytes=ENTER * MIB),
        cost_estimate=pl.CostEstimate(flops=0, bytes_accessed=0, transcendentals=0),
        name="enter",
    )(tokens, turned)


def quarters(ref, start, count):
    return ref[start : start + count].astype(jnp.float32)


def on_first():
    return lax.axis_index("wt") < 2


def apart(kept, got, mine_ref, send_ref):
    first = jnp.concatenate([kept[0], got[0]], axis=0)
    second = jnp.concatenate([kept[1], got[1]], axis=0)
    mine_ref[...] = jnp.where(on_first(), first, second).astype(mine_ref.dtype)
    send_ref[...] = jnp.where(on_first(), second, first).astype(send_ref.dtype)


def part_kernel(kept_ref, got_ref, mine_ref, send_ref):
    share = mine_ref.shape[1]
    halves = [[ref[:, :share].astype(jnp.float32), ref[:, share:].astype(jnp.float32)] for ref in (kept_ref, got_ref)]
    apart(*halves, mine_ref, send_ref)


def near_kernel(mine_ref, theirs_ref, out_ref):
    count = mine_ref.shape[0] // 2
    pieces = []
    for start in (0, count):
        mine, theirs = quarters(mine_ref, start, count), quarters(theirs_ref, start, count)
        pieces += [jnp.where(on_first(), mine, theirs), jnp.where(on_first(), theirs, mine)]
    out_ref[...] = jnp.concatenate(pieces, axis=0).astype(out_ref.dtype)


def leave_kernel(shares_ref, tokens_ref, mod_ref, bias_ref, out_ref):
    share = shares_ref.shape[2]
    for n in range(4):
        lanes = slice(n * share, (n + 1) * share)
        branch = sum(shares_ref[4 * place + n].astype(jnp.float32) for place in range(4)) + bias_ref[:, lanes]
        out_ref[0, :, lanes] = (tokens_ref[0, :, lanes].astype(jnp.float32) + mod_ref[2, :, lanes] * branch).astype(out_ref.dtype)


def small(kernel, outs, *args, beside=0):
    return pl.pallas_call(
        kernel,
        out_shape=outs,
        compiler_params=pltpu.CompilerParams(vmem_limit_bytes=4 * MIB),
        cost_estimate=pl.CostEstimate(flops=400 * beside, bytes_accessed=beside, transcendentals=beside // 100) if beside else None,
        name=kernel.__name__,
    )(*args)


def pick_lanes(blocks, lanes):
    return (
        lax.broadcasted_iota(jnp.int32, (blocks, lanes), 1) // BLOCK
        == lax.broadcasted_iota(jnp.int32, (blocks, lanes), 0)
    ).astype(jnp.bfloat16)


def prune_kernel(mask_dim, mask_ref, weight_ref, out_ref, lanes):
    lanes[...] = lax.dot_general(
        mask_ref[...].astype(jnp.bfloat16),
        pick_lanes(mask_ref.shape[mask_dim], out_ref.shape[1]),
        (((mask_dim,), (0,)), ((), ())),
        preferred_element_type=jnp.float32,
    )

    def body(b, _):
        rows = pl.ds(pl.multiple_of(b * BLOCK, BLOCK), BLOCK)
        out_ref[rows, :] = weight_ref[rows, :] * lanes[pl.ds(b, 1), :].astype(jnp.bfloat16)
        return 0

    lax.fori_loop(0, out_ref.shape[0] // BLOCK, body, 0)


def prune(weight, mask, turned, hint=1):
    size = 2 * weight.size
    return pl.pallas_call(
        functools.partial(prune_kernel, 0 if turned else 1),
        out_shape=jax.ShapeDtypeStruct(weight.shape, jnp.bfloat16),
        scratch_shapes=[pltpu.VMEM((weight.shape[0] // BLOCK, weight.shape[1]), jnp.float32)],
        compiler_params=pltpu.CompilerParams(vmem_limit_bytes=14 * MIB),
        cost_estimate=pl.CostEstimate(flops=size * hint, bytes_accessed=2 * size * hint, transcendentals=0),
        name="prune",
    )(mask.T if turned else mask, weight)


def in_kernel(count, x_ref, *refs):
    weights, (keep_ref, send_ref) = refs[:count], refs[count:]
    rows, share = x_ref.shape
    x = x_ref[...]
    tiles = []
    for ref in weights:
        if len(ref.shape) == 3:
            tiles += [(ref, n) for n in range(ref.shape[0])]
        else:
            tiles += [(ref, (slice(None), slice(n, n + share))) for n in range(0, ref.shape[1], share)]
    for n, (ref, place) in enumerate(tiles):
        lanes = slice(n * share, (n + 1) * share)
        out = jnp.dot(x, ref[place], preferred_element_type=jnp.float32)
        keep_ref[:, lanes] = jnp.concatenate([out[r : r + 8] for r in range(0, rows, 16)], axis=0)
        send_ref[:, lanes] = jnp.concatenate([out[r + 8 : r + 16] for r in range(0, rows, 16)], axis=0).astype(jnp.bfloat16)


def in_products(x, *weights, hint=1):
    rows, depth = x.shape
    size = sum(w.size for w in weights)
    return pl.pallas_call(
        functools.partial(in_kernel, len(weights)),
        out_shape=[
            jax.ShapeDtypeStruct((rows // 2, size // depth), jnp.float32),
            jax.ShapeDtypeStruct((rows // 2, size // depth), jnp.bfloat16),
        ],
        compiler_params=pltpu.CompilerParams(vmem_limit_bytes=12 * MIB),
        cost_estimate=pl.CostEstimate(flops=2 * rows * size * hint, bytes_accessed=2 * size * hint, transcendentals=0),
        name="in_products",
    )(x, *weights)


def total_kernel(start, near_kept, near_got, far_kept, far_got, total_ref, send_ref):
    lanes = slice(start, start + total_ref.shape[1])
    half = near_kept.shape[0]
    for rows, kept, got in (
        (slice(0, half), near_kept[:, lanes], near_got[:, lanes]),
        (slice(half, 2 * half), far_kept[...], far_got[...]),
    ):
        total = kept + got.astype(jnp.float32)
        total_ref[rows] = total
        send_ref[rows] = total.astype(jnp.bfloat16)


def over_cores(start, near, far):
    shape = (2 * far[0].shape[0], far[0].shape[1])
    return pl.pallas_call(
        functools.partial(total_kernel, start),
        out_shape=[jax.ShapeDtypeStruct(shape, jnp.float32), jax.ShapeDtypeStruct(shape, jnp.bfloat16)],
        compiler_params=pltpu.CompilerParams(vmem_limit_bytes=8 * MIB),
        name="over_cores",
    )(*near, *far)


def attend_kernel(images, part, own_ref, other_ref, bias_ref, gains_ref, out_ref):
    rows, share = out_ref.shape
    heads = share // HEAD

    def stacked(which):
        lanes = slice(which * share, (which + 1) * share)
        flat = own_ref[:, lanes] + other_ref[:, lanes].astype(jnp.float32)
        flat = (flat + bias_ref[which : which + 1, :]).astype(jnp.bfloat16)
        return jnp.concatenate([flat[:, h * HEAD : (h + 1) * HEAD] for h in range(heads)], axis=0)

    def normed(which):
        wide = stacked(which).astype(jnp.float32)
        scale = lax.rsqrt(jnp.mean(wide * wide, axis=-1, keepdims=True) + 1e-06)
        return (wide * scale * gains_ref[which : which + 1, :]).astype(jnp.bfloat16)

    queries, keys, values = normed(0), normed(1), stacked(2)
    scores = lax.dot_general(
        queries, keys, (((1,), (1,)), ((), ())), preferred_element_type=jnp.float32
    ) * (1.0 / math.sqrt(HEAD))
    size = heads * rows

    def group(dim):
        place = lax.broadcasted_iota(jnp.int32, (size, size), dim)
        return place // rows * images + place // part % images

    same = group(0) == group(1)
    weights = jnp.where(same, jnp.exp(jnp.where(same, scores, 0.0)), 0.0)
    denoms = jnp.sum(weights, axis=-1, keepdims=True)
    summed = jnp.dot(weights.astype(jnp.bfloat16), values, preferred_element_type=jnp.float32)
    attended = (summed / denoms).astype(jnp.bfloat16)
    for h in range(heads):
        out_ref[:, h * HEAD : (h + 1) * HEAD] = attended[h * rows : (h + 1) * rows]


def attention(images, part, own, other, bias, gains):
    return pl.pallas_call(
        functools.partial(attend_kernel, images, part),
        out_shape=jax.ShapeDtypeStruct((own.shape[0], bias.shape[1]), jnp.bfloat16),
        compiler_params=pltpu.CompilerParams(vmem_limit_bytes=8 * MIB),
        name="attention",
    )(own, other, bias, gains)


def hidden_kernel(own_ref, other_ref, bias_ref, out_ref):
    step = 6 * HEAD
    for start in range(0, out_ref.shape[1], step):
        lanes = slice(start, start + step)
        v = own_ref[:, lanes] + other_ref[:, lanes].astype(jnp.float32) + bias_ref[:, lanes]
        cubic = math.sqrt(2.0 / math.pi) * (v + 0.044715 * (v * v * v))
        out_ref[:, lanes] = (0.5 * v * (1.0 + jnp.tanh(cubic))).astype(jnp.bfloat16)


def activate(own, other, bias):
    return pl.pallas_call(
        hidden_kernel,
        out_shape=jax.ShapeDtypeStruct(own.shape, jnp.bfloat16),
        compiler_params=pltpu.CompilerParams(vmem_limit_bytes=8 * MIB),
        name="hidden",
    )(own, other, bias.reshape(1, -1))


def out_kernel(a_mine, a_theirs, h_mine, h_theirs, proj_ref, down_ref, out_ref):
    attended = jnp.concatenate([a_mine[...], a_theirs[...]], axis=0)
    hidden = jnp.concatenate([h_mine[...], h_theirs[...]], axis=0)
    total = jnp.dot(attended, proj_ref[...], preferred_element_type=jnp.float32)
    total += jnp.dot(hidden, down_ref[...], preferred_element_type=jnp.float32)
    place, core = lax.axis_index("seq"), lax.axis_index("wt") % 2
    count = out_ref.shape[1]
    row = 0
    for other_core in range(2):
        for step in NEAR_FIRST:
            for chip in range(2):
                target = (place ^ step) * 4 + 2 * chip + (core ^ other_core)
                out_ref[target] = total[row : row + count].astype(out_ref.dtype)
                row += count


def out_products(count, mine, theirs, hidden, hidden_theirs, proj, down):
    half, width = mine.shape[0], proj.shape[1]
    size = proj.size + down.size
    return pl.pallas_call(
        out_kernel,
        out_shape=jax.ShapeDtypeStruct((2 * half // count, count, width), jnp.bfloat16),
        compiler_params=pltpu.CompilerParams(vmem_limit_bytes=12 * MIB),
        cost_estimate=pl.CostEstimate(flops=4 * half * size, bytes_accessed=2 * size, transcendentals=0),
        name="out_products",
    )(mine, theirs, hidden, hidden_theirs, proj, down)


def swap(values, axis, bit):
    count = lax.axis_size(axis)
    return lax.ppermute(values, axis, [(i, i ^ bit) for i in range(count)])


def fixed_shards(
    tokens,
    modulation,
    qkv_weight,
    qkv_bias,
    norm_gains,
    up_weight,
    up_mask,
    up_bias,
    proj_weight,
    down_weight,
    down_mask,
    out_bias,
):
    count, features = tokens.shape[1:]
    share = features // 4
    bf16 = jnp.bfloat16

    def rows_of(n, kind):
        return jax.ShapeDtypeStruct((n * count, share), kind)

    kept, given = enter(tokens, modulation)
    mine, given = small(part_kernel, [rows_of(2, bf16)] * 2, kept, swap(given, "wt", 1), beside=BESIDE)
    near = small(near_kernel, rows_of(4, bf16), mine, swap(given, "wt", 2), beside=BESIDE)
    up_pruned = prune(up_weight, up_mask, False)
    near, up_pruned = lax.optimization_barrier((near, up_pruned))
    near = jnp.concatenate([near, swap(near, "seq", 2)], axis=0)
    far = swap(near, "seq", 1)

    def with_theirs(kept, values):
        return kept, swap(values, "wt", 1)

    qkv = qkv_weight.transpose(1, 0, 2)
    kept, given = in_products(near, qkv, up_pruned)
    given, far = lax.optimization_barrier((given, far))
    near_sums = with_theirs(kept, given)
    kept, given = in_products(far, qkv, hint=0)
    far, given = lax.optimization_barrier((far, given))
    own, sent = over_cores(0, near_sums, with_theirs(kept, given))
    qkv_pair = own, swap(sent, "wt", 2)
    own, sent = over_cores(own.shape[1], near_sums, with_theirs(*in_products(far, up_pruned, hint=0)))
    up_pair = own, swap(sent, "wt", 2)
    down_pruned = prune(down_weight, down_mask, True, hint=0)
    qkv_pair, down_pruned = lax.optimization_barrier((qkv_pair, down_pruned))
    attended = attention(2, count, *qkv_pair, qkv_bias, norm_gains)
    hidden = activate(*up_pair, up_bias)
    shares = out_products(
        count, attended, swap(attended, "wt", 1), hidden, swap(hidden, "wt", 1), proj_weight, down_pruned
    )
    shares = lax.all_to_all(shares, ("seq", "wt"), split_axis=0, concat_axis=0, tiled=True)
    out = jax.ShapeDtypeStruct(tokens.shape, tokens.dtype)
    return small(leave_kernel, out, shares, tokens, modulation.transpose(1, 0, 2), out_bias.reshape(1, -1))


def solution(mesh):
    seq, wt = mesh.shape["seq"], mesh.shape["wt"]

    def shards(*args):
        share = args[2].shape[2]
        whole_heads = share % HEAD == 0 and share == args[8].shape[1] and args[5].shape[1] % share == 0
        fits = whole_heads and wt == 4 and seq == 4 and args[0].shape[1] == 4
        return (fixed_shards if fits else gathered_shards)(*args)

    return jax.shard_map(
        shards,
        mesh=mesh,
        in_specs=(
            P(("rep", "wt"), "seq", None),
            P(("rep", "wt"), None, None),
            P("wt", None, "seq"),
            P(None, "seq"),
            P(),
            P("wt", "seq"),
            P("wt", "seq"),
            P("seq"),
            P("seq", "wt"),
            P("seq", "wt"),
            P("seq", "wt"),
            P(),
        ),
        out_specs=P(("rep", "wt"), "seq", None),
        check_vma=False,
    )
```

```python
import functools
import math

import jax
import jax.numpy as jnp
from jax import lax
from jax.experimental import pallas as pl
from jax.experimental.pallas import tpu as pltpu
from jax.sharding import PartitionSpec as P

HEAD = 128
BLOCK = 64
MIB = 1024 * 1024
STREAM = 52
AHEAD = 7
BESIDE = 16 * MIB


def masked(weight, keep_mask):
    row_blocks, col_blocks = keep_mask.shape
    expanded = jnp.broadcast_to(keep_mask[:, None, :, None], (row_blocks, BLOCK, col_blocks, BLOCK))
    return weight * expanded.reshape(weight.shape).astype(jnp.bfloat16)


def layer_norm(values):
    center = values - jnp.mean(values, axis=-1, keepdims=True)
    spread = jnp.mean(center * center, axis=-1, keepdims=True)
    return center * lax.rsqrt(spread + 1e-06)


def norm_heads(flat_rows, gains):
    shaped_rows = flat_rows.reshape(flat_rows.shape[0], -1, HEAD).astype(jnp.float32)
    scaled = (
        shaped_rows
        * lax.rsqrt(jnp.mean(shaped_rows * shaped_rows, axis=-1, keepdims=True) + 1e-06)
        * gains
    )
    return scaled.astype(jnp.bfloat16)


def attend(queries, keys_normed, values):
    scores = jnp.einsum(
        "qhd,khd->hqk", queries, keys_normed, preferred_element_type=jnp.float32
    ) / math.sqrt(HEAD)
    weights = jnp.exp(scores)
    denoms = jnp.sum(weights, axis=2)
    summed = jnp.einsum(
        "hqk,khd->qhd", weights.astype(jnp.bfloat16), values, preferred_element_type=jnp.float32
    )
    return (summed, denoms)


def gathered_shards(
    tokens,
    modulation,
    qkv_weight,
    qkv_bias,
    norm_gains,
    up_weight,
    up_mask,
    up_bias,
    proj_weight,
    down_weight,
    down_mask,
    out_bias,
):
    own_rows = tokens[0]
    mod_rows = modulation[0]
    row_count = own_rows.shape[0]
    feature_count = own_rows.shape[1]
    head_count = feature_count // HEAD
    normed = layer_norm(own_rows.astype(jnp.float32))
    shaped = ((1.0 + mod_rows[1]) * normed + mod_rows[0]).astype(jnp.bfloat16)
    gathered = lax.all_gather(shaped, "seq", axis=0, tiled=True)
    seq_len = gathered.shape[0]
    col_share = qkv_weight.shape[2]
    up_local = masked(up_weight, up_mask)
    pieces = (
        lax.all_gather(qkv_weight, "wt", axis=0, tiled=True),
        lax.all_gather(up_local, "wt", axis=0, tiled=True),
    )
    piece_rows = pieces[0].shape[0]
    first = jnp.dot(
        gathered, pieces[0].reshape(piece_rows, 3 * col_share), preferred_element_type=jnp.float32
    )
    second = jnp.dot(gathered, pieces[1], preferred_element_type=jnp.float32)
    qkv_local = (first.reshape(seq_len, 3, col_share) + qkv_bias).astype(jnp.bfloat16)
    hidden = jax.nn.gelu(second + up_bias, approximate=True).astype(jnp.bfloat16)
    query_flat = lax.all_to_all(qkv_local[:, 0, :], "seq", split_axis=0, concat_axis=1, tiled=True)
    kv_whole = lax.all_gather(qkv_local[:, 1:, :], "seq", axis=2, tiled=True)
    queries = norm_heads(query_flat, norm_gains[0])
    keys_normed = norm_heads(kv_whole[:, 0, :], norm_gains[1])
    values = kv_whole[:, 1, :].reshape(seq_len, head_count, HEAD)
    summed, denoms = attend(queries, keys_normed, values)
    attended = (
        (summed / denoms.T[:, :, None]).reshape(row_count, feature_count).astype(jnp.bfloat16)
    )
    attended_cols = lax.all_to_all(attended, "seq", split_axis=1, concat_axis=0, tiled=True)
    down_local = masked(down_weight, down_mask)
    proj_full, down_full = (
        lax.all_gather(proj_weight, "wt", axis=1, tiled=True),
        lax.all_gather(down_local, "wt", axis=1, tiled=True),
    )
    branch_sum = lax.psum_scatter(
        jnp.dot(attended_cols, proj_full, preferred_element_type=jnp.float32)
        + jnp.dot(hidden, down_full, preferred_element_type=jnp.float32),
        "seq",
        scatter_dimension=0,
        tiled=True,
    )
    result = own_rows.astype(jnp.float32) + mod_rows[2] * (branch_sum + out_bias)
    return result.astype(jnp.bfloat16)[None]


def enter_kernel(tokens_ref, mod_ref, out_ref):
    shaped = (1.0 + mod_ref[1]) * layer_norm(tokens_ref[0].astype(jnp.float32)) + mod_ref[0]
    shaped = shaped.astype(jnp.bfloat16)
    share = out_ref.shape[2]
    for place in range(out_ref.shape[0]):
        out_ref[place] = shaped[:, place % 4 * share : (place % 4 + 1) * share]


def enter(tokens, modulation):
    _, count, features = tokens.shape
    return pl.pallas_call(
        enter_kernel,
        out_shape=jax.ShapeDtypeStruct((16, count, features // 4), jnp.bfloat16),
        compiler_params=pltpu.CompilerParams(vmem_limit_bytes=4 * MIB),
        cost_estimate=pl.CostEstimate(flops=400 * BESIDE, bytes_accessed=BESIDE, transcendentals=BESIDE // 100),
        name="enter",
    )(tokens, modulation.transpose(1, 0, 2))


def leave_kernel(shares_ref, tokens_ref, mod_ref, bias_ref, out_ref):
    share = shares_ref.shape[2]
    for n in range(4):
        lanes = slice(n * share, (n + 1) * share)
        branch = sum(shares_ref[4 * place + n].astype(jnp.float32) for place in range(4)) + bias_ref[:, lanes]
        out_ref[0, :, lanes] = (tokens_ref[0, :, lanes].astype(jnp.float32) + mod_ref[2, :, lanes] * branch).astype(out_ref.dtype)


def small(kernel, outs, *args):
    return pl.pallas_call(
        kernel,
        out_shape=outs,
        compiler_params=pltpu.CompilerParams(vmem_limit_bytes=4 * MIB),
        name=kernel.__name__,
    )(*args)


def pick_lanes(blocks, lanes):
    return (
        lax.broadcasted_iota(jnp.int32, (blocks, lanes), 1) // BLOCK
        == lax.broadcasted_iota(jnp.int32, (blocks, lanes), 0)
    ).astype(jnp.bfloat16)


def prune_kernel(mask_dim, mask_ref, weight_ref, out_ref, lanes):
    lanes[...] = lax.dot_general(
        mask_ref[...].astype(jnp.bfloat16),
        pick_lanes(mask_ref.shape[mask_dim], out_ref.shape[1]),
        (((mask_dim,), (0,)), ((), ())),
        preferred_element_type=jnp.float32,
    )

    def body(b, _):
        rows = pl.ds(pl.multiple_of(b * BLOCK, BLOCK), BLOCK)
        out_ref[rows, :] = weight_ref[rows, :] * lanes[pl.ds(b, 1), :].astype(jnp.bfloat16)
        return 0

    lax.fori_loop(0, out_ref.shape[0] // BLOCK, body, 0)


def prune(weight, mask, turned, hint=1):
    size = 2 * weight.size
    return pl.pallas_call(
        functools.partial(prune_kernel, 0 if turned else 1),
        out_shape=jax.ShapeDtypeStruct(weight.shape, jnp.bfloat16),
        scratch_shapes=[pltpu.VMEM((weight.shape[0] // BLOCK, weight.shape[1]), jnp.float32)],
        compiler_params=pltpu.CompilerParams(vmem_limit_bytes=14 * MIB),
        cost_estimate=pl.CostEstimate(flops=size * hint, bytes_accessed=2 * size * hint, transcendentals=0),
        name="prune",
    )(mask.T if turned else mask, weight)


def in_kernel(got_ref, mask_hbm, qkv_hbm, up_hbm, keep_ref, send_ref, tiles, mask_ref, lanes, sems):
    share = got_ref.shape[2]
    count = tiles.shape[0]
    copies = [
        pltpu.make_async_copy(
            qkv_hbm.at[n] if n < 3 else up_hbm.at[:, pl.ds((n - 3) * share, share)], tiles.at[n], sems.at[n]
        )
        for n in range(count)
    ]
    mask_copy = pltpu.make_async_copy(mask_hbm, mask_ref, sems.at[count])
    mask_copy.start()
    for copy in copies[:AHEAD]:
        copy.start()
    mask_copy.wait()
    lanes[...] = jnp.dot(
        mask_ref[...].astype(jnp.bfloat16),
        pick_lanes(mask_ref.shape[1], lanes.shape[1]),
        preferred_element_type=jnp.float32,
    )
    core = lax.axis_index("wt") % 2
    x = jnp.concatenate(
        [
            got_ref[4 * place + 2 * chip + (core ^ other_core)].astype(jnp.float32)
            for place in range(4)
            for other_core in range(2)
            for chip in range(2)
        ],
        axis=0,
    ).astype(jnp.bfloat16)
    for n, copy in enumerate(copies):
        copy.wait()
        if n + AHEAD < count:
            copies[n + AHEAD].start()
        if n < 3:
            weight = tiles[n]
        else:
            cols = slice((n - 3) * share, (n - 2) * share)
            weight = jnp.concatenate(
                [
                    tiles[n, r * BLOCK : (r + 1) * BLOCK] * lanes[r : r + 1, cols].astype(jnp.bfloat16)
                    for r in range(lanes.shape[0])
                ],
                axis=0,
            )
        out = jnp.dot(x, weight, preferred_element_type=jnp.float32)
        cols = slice(n * share, (n + 1) * share)
        keep_ref[:, cols] = jnp.concatenate([out[r : r + 8] for r in range(0, 64, 16)], axis=0)
        send_ref[:, cols] = jnp.concatenate([out[r + 8 : r + 16] for r in range(0, 64, 16)], axis=0).astype(jnp.bfloat16)


def in_products(got, qkv_weight, up_weight, up_mask):
    places, count, depth = got.shape
    size = qkv_weight.size + up_weight.size
    half, width = places * count // 2, size // depth
    return pl.pallas_call(
        in_kernel,
        in_specs=[pl.BlockSpec(memory_space=pltpu.VMEM)] + [pl.BlockSpec(memory_space=pltpu.HBM)] * 3,
        out_shape=[
            jax.ShapeDtypeStruct((half, width), jnp.float32),
            jax.ShapeDtypeStruct((half, width), jnp.bfloat16),
        ],
        scratch_shapes=[
            pltpu.VMEM((width // depth, depth, depth), jnp.bfloat16),
            pltpu.VMEM(up_mask.shape, up_mask.dtype),
            pltpu.VMEM((up_mask.shape[0], up_weight.shape[1]), jnp.float32),
            pltpu.SemaphoreType.DMA((width // depth + 1,)),
        ],
        compiler_params=pltpu.CompilerParams(vmem_limit_bytes=STREAM * MIB),
        cost_estimate=pl.CostEstimate(flops=4 * half * size, bytes_accessed=2 * size, transcendentals=0),
        name="in_products",
    )(got, up_mask, qkv_weight.transpose(1, 0, 2), up_weight)


def mid_kernel(images, part, own_ref, other_ref, qkv_bias_ref, gains_ref, up_bias_ref, out_ref):
    rows = own_ref.shape[0]
    share = qkv_bias_ref.shape[1]
    heads = share // HEAD

    def total(start, size):
        return own_ref[:, start : start + size] + other_ref[:, start : start + size].astype(jnp.float32)

    def stacked(which):
        flat = (total(which * share, share) + qkv_bias_ref[which : which + 1, :]).astype(jnp.bfloat16)
        return jnp.concatenate([flat[:, h * HEAD : (h + 1) * HEAD] for h in range(heads)], axis=0)

    def normed(which):
        wide = stacked(which).astype(jnp.float32)
        scale = lax.rsqrt(jnp.mean(wide * wide, axis=-1, keepdims=True) + 1e-06)
        return (wide * scale * gains_ref[which : which + 1, :]).astype(jnp.bfloat16)

    queries, keys, values = normed(0), normed(1), stacked(2)
    scores = lax.dot_general(
        queries, keys, (((1,), (1,)), ((), ())), preferred_element_type=jnp.float32
    ) * (1.0 / math.sqrt(HEAD))
    size = heads * rows

    def group(dim):
        place = lax.broadcasted_iota(jnp.int32, (size, size), dim)
        return place // rows * images + place // part % images

    same = group(0) == group(1)
    weights = jnp.where(same, jnp.exp(jnp.where(same, scores, 0.0)), 0.0)
    denoms = jnp.sum(weights, axis=-1, keepdims=True)
    summed = jnp.dot(weights.astype(jnp.bfloat16), values, preferred_element_type=jnp.float32)
    attended = (summed / denoms).astype(jnp.bfloat16)
    for h in range(heads):
        out_ref[:, h * HEAD : (h + 1) * HEAD] = attended[h * rows : (h + 1) * rows]
    hidden = out_ref.shape[1] - share
    for start in range(0, hidden, share):
        v = total(3 * share + start, share) + up_bias_ref[:, start : start + share]
        cubic = math.sqrt(2.0 / math.pi) * (v + 0.044715 * (v * v * v))
        out_ref[:, share + start : 2 * share + start] = (0.5 * v * (1.0 + jnp.tanh(cubic))).astype(jnp.bfloat16)


def middle(images, part, own, other, qkv_bias, gains, up_bias):
    rows = own.shape[0]
    share = qkv_bias.shape[1]
    width = own.shape[1] - 2 * share
    return pl.pallas_call(
        functools.partial(mid_kernel, images, part),
        out_shape=jax.ShapeDtypeStruct((rows, width), jnp.bfloat16),
        compiler_params=pltpu.CompilerParams(vmem_limit_bytes=8 * MIB),
        name="middle",
    )(own, other, qkv_bias, gains, up_bias.reshape(1, -1))


def out_kernel(mine, theirs, proj_ref, down_ref, out_ref):
    mixed = jnp.concatenate([mine[...], theirs[...]], axis=0)
    depth = proj_ref.shape[0]
    total = jnp.dot(mixed[:, :depth], proj_ref[...], preferred_element_type=jnp.float32)
    total += jnp.dot(mixed[:, depth:], down_ref[...], preferred_element_type=jnp.float32)
    core = lax.axis_index("wt") % 2
    count = out_ref.shape[1]
    row = 0
    for other_core in range(2):
        for place in range(4):
            for chip in range(2):
                target = 4 * place + 2 * chip + (core ^ other_core)
                out_ref[target] = total[row : row + count].astype(out_ref.dtype)
                row += count


def out_products(count, mine, theirs, proj, down):
    half, width = mine.shape[0], proj.shape[1]
    size = proj.size + down.size
    return pl.pallas_call(
        out_kernel,
        out_shape=jax.ShapeDtypeStruct((2 * half // count, count, width), jnp.bfloat16),
        compiler_params=pltpu.CompilerParams(vmem_limit_bytes=12 * MIB),
        cost_estimate=pl.CostEstimate(flops=4 * half * size, bytes_accessed=2 * size, transcendentals=0),
        name="out_products",
    )(mine, theirs, proj, down)


def swap(values, axis, bit):
    count = lax.axis_size(axis)
    return lax.ppermute(values, axis, [(i, i ^ bit) for i in range(count)])


def fixed_shards(
    tokens,
    modulation,
    qkv_weight,
    qkv_bias,
    norm_gains,
    up_weight,
    up_mask,
    up_bias,
    proj_weight,
    down_weight,
    down_mask,
    out_bias,
):
    count = tokens.shape[1]
    both = ("seq", "wt")
    got = lax.all_to_all(enter(tokens, modulation), both, split_axis=0, concat_axis=0, tiled=True)
    kept, given = in_products(got, qkv_weight, up_weight, up_mask)
    own = kept + swap(given, "wt", 1).astype(jnp.float32)
    pair = own, swap(own.astype(jnp.bfloat16), "wt", 2)
    down_pruned = prune(down_weight, down_mask, True, hint=0)
    pair, down_pruned = lax.optimization_barrier((pair, down_pruned))
    mixed = middle(2, count, *pair, qkv_bias, norm_gains, up_bias)
    shares = out_products(count, mixed, swap(mixed, "wt", 1), proj_weight, down_pruned)
    shares = lax.all_to_all(shares, both, split_axis=0, concat_axis=0, tiled=True)
    out = jax.ShapeDtypeStruct(tokens.shape, tokens.dtype)
    return small(leave_kernel, out, shares, tokens, modulation.transpose(1, 0, 2), out_bias.reshape(1, -1))


def solution(mesh):
    seq, wt = mesh.shape["seq"], mesh.shape["wt"]

    def shards(*args):
        share = args[2].shape[2]
        whole_heads = share % HEAD == 0 and share == args[8].shape[1] and args[5].shape[1] % share == 0
        fits = whole_heads and wt == 4 and seq == 4 and args[0].shape[1] == 4
        return (fixed_shards if fits else gathered_shards)(*args)

    return jax.shard_map(
        shards,
        mesh=mesh,
        in_specs=(
            P(("rep", "wt"), "seq", None),
            P(("rep", "wt"), None, None),
            P("wt", None, "seq"),
            P(None, "seq"),
            P(),
            P("wt", "seq"),
            P("wt", "seq"),
            P("seq"),
            P("seq", "wt"),
            P("seq", "wt"),
            P("seq", "wt"),
            P(),
        ),
        out_specs=P(("rep", "wt"), "seq", None),
        check_vma=False,
    )
```

```python
import functools
import math

import jax
import jax.numpy as jnp
from jax import lax
from jax.experimental import pallas as pl
from jax.experimental.pallas import tpu as pltpu
from jax.sharding import PartitionSpec as P

HEAD = 128
BLOCK = 64
MIB = 1024 * 1024
STREAM = 52
BESIDE = 16 * MIB


def masked(weight, keep_mask):
    row_blocks, col_blocks = keep_mask.shape
    expanded = jnp.broadcast_to(keep_mask[:, None, :, None], (row_blocks, BLOCK, col_blocks, BLOCK))
    return weight * expanded.reshape(weight.shape).astype(jnp.bfloat16)


def layer_norm(values):
    center = values - jnp.mean(values, axis=-1, keepdims=True)
    spread = jnp.mean(center * center, axis=-1, keepdims=True)
    return center * lax.rsqrt(spread + 1e-06)


def norm_heads(flat_rows, gains):
    shaped_rows = flat_rows.reshape(flat_rows.shape[0], -1, HEAD).astype(jnp.float32)
    scaled = (
        shaped_rows
        * lax.rsqrt(jnp.mean(shaped_rows * shaped_rows, axis=-1, keepdims=True) + 1e-06)
        * gains
    )
    return scaled.astype(jnp.bfloat16)


def attend(queries, keys_normed, values):
    scores = jnp.einsum(
        "qhd,khd->hqk", queries, keys_normed, preferred_element_type=jnp.float32
    ) / math.sqrt(HEAD)
    weights = jnp.exp(scores)
    denoms = jnp.sum(weights, axis=2)
    summed = jnp.einsum(
        "hqk,khd->qhd", weights.astype(jnp.bfloat16), values, preferred_element_type=jnp.float32
    )
    return (summed, denoms)


def gathered_shards(
    tokens,
    modulation,
    qkv_weight,
    qkv_bias,
    norm_gains,
    up_weight,
    up_mask,
    up_bias,
    proj_weight,
    down_weight,
    down_mask,
    out_bias,
):
    own_rows = tokens[0]
    mod_rows = modulation[0]
    row_count = own_rows.shape[0]
    feature_count = own_rows.shape[1]
    head_count = feature_count // HEAD
    normed = layer_norm(own_rows.astype(jnp.float32))
    shaped = ((1.0 + mod_rows[1]) * normed + mod_rows[0]).astype(jnp.bfloat16)
    gathered = lax.all_gather(shaped, "seq", axis=0, tiled=True)
    seq_len = gathered.shape[0]
    col_share = qkv_weight.shape[2]
    up_local = masked(up_weight, up_mask)
    pieces = (
        lax.all_gather(qkv_weight, "wt", axis=0, tiled=True),
        lax.all_gather(up_local, "wt", axis=0, tiled=True),
    )
    piece_rows = pieces[0].shape[0]
    first = jnp.dot(
        gathered, pieces[0].reshape(piece_rows, 3 * col_share), preferred_element_type=jnp.float32
    )
    second = jnp.dot(gathered, pieces[1], preferred_element_type=jnp.float32)
    qkv_local = (first.reshape(seq_len, 3, col_share) + qkv_bias).astype(jnp.bfloat16)
    hidden = jax.nn.gelu(second + up_bias, approximate=True).astype(jnp.bfloat16)
    query_flat = lax.all_to_all(qkv_local[:, 0, :], "seq", split_axis=0, concat_axis=1, tiled=True)
    kv_whole = lax.all_gather(qkv_local[:, 1:, :], "seq", axis=2, tiled=True)
    queries = norm_heads(query_flat, norm_gains[0])
    keys_normed = norm_heads(kv_whole[:, 0, :], norm_gains[1])
    values = kv_whole[:, 1, :].reshape(seq_len, head_count, HEAD)
    summed, denoms = attend(queries, keys_normed, values)
    attended = (
        (summed / denoms.T[:, :, None]).reshape(row_count, feature_count).astype(jnp.bfloat16)
    )
    attended_cols = lax.all_to_all(attended, "seq", split_axis=1, concat_axis=0, tiled=True)
    down_local = masked(down_weight, down_mask)
    proj_full, down_full = (
        lax.all_gather(proj_weight, "wt", axis=1, tiled=True),
        lax.all_gather(down_local, "wt", axis=1, tiled=True),
    )
    branch_sum = lax.psum_scatter(
        jnp.dot(attended_cols, proj_full, preferred_element_type=jnp.float32)
        + jnp.dot(hidden, down_full, preferred_element_type=jnp.float32),
        "seq",
        scatter_dimension=0,
        tiled=True,
    )
    result = own_rows.astype(jnp.float32) + mod_rows[2] * (branch_sum + out_bias)
    return result.astype(jnp.bfloat16)[None]


def enter_kernel(tokens_ref, mod_ref, out_ref):
    shaped = (1.0 + mod_ref[1]) * layer_norm(tokens_ref[0].astype(jnp.float32)) + mod_ref[0]
    shaped = shaped.astype(jnp.bfloat16)
    share = out_ref.shape[2]
    for place in range(out_ref.shape[0]):
        out_ref[place] = shaped[:, place % 4 * share : (place % 4 + 1) * share]


def enter(tokens, modulation):
    _, count, features = tokens.shape
    return pl.pallas_call(
        enter_kernel,
        out_shape=jax.ShapeDtypeStruct((16, count, features // 4), jnp.bfloat16),
        compiler_params=pltpu.CompilerParams(vmem_limit_bytes=4 * MIB),
        cost_estimate=pl.CostEstimate(flops=400 * BESIDE, bytes_accessed=BESIDE, transcendentals=BESIDE // 100),
        name="enter",
    )(tokens, modulation.transpose(1, 0, 2))


def leave_kernel(shares_ref, tokens_ref, mod_ref, bias_ref, out_ref):
    share = shares_ref.shape[2]
    for n in range(4):
        lanes = slice(n * share, (n + 1) * share)
        branch = sum(shares_ref[4 * place + n].astype(jnp.float32) for place in range(4)) + bias_ref[:, lanes]
        out_ref[0, :, lanes] = (tokens_ref[0, :, lanes].astype(jnp.float32) + mod_ref[2, :, lanes] * branch).astype(out_ref.dtype)


def small(kernel, outs, *args):
    return pl.pallas_call(
        kernel,
        out_shape=outs,
        compiler_params=pltpu.CompilerParams(vmem_limit_bytes=4 * MIB),
        name=kernel.__name__,
    )(*args)


def pick_lanes(blocks, lanes):
    return (
        lax.broadcasted_iota(jnp.int32, (blocks, lanes), 1) // BLOCK
        == lax.broadcasted_iota(jnp.int32, (blocks, lanes), 0)
    ).astype(jnp.bfloat16)


def prune_kernel(mask_dim, mask_ref, weight_ref, out_ref, lanes):
    lanes[...] = lax.dot_general(
        mask_ref[...].astype(jnp.bfloat16),
        pick_lanes(mask_ref.shape[mask_dim], out_ref.shape[1]),
        (((mask_dim,), (0,)), ((), ())),
        preferred_element_type=jnp.float32,
    )

    def body(b, _):
        rows = pl.ds(pl.multiple_of(b * BLOCK, BLOCK), BLOCK)
        out_ref[rows, :] = weight_ref[rows, :] * lanes[pl.ds(b, 1), :].astype(jnp.bfloat16)
        return 0

    lax.fori_loop(0, out_ref.shape[0] // BLOCK, body, 0)


def prune(weight, mask, turned, hint=1):
    size = 2 * weight.size
    return pl.pallas_call(
        functools.partial(prune_kernel, 0 if turned else 1),
        out_shape=jax.ShapeDtypeStruct(weight.shape, jnp.bfloat16),
        scratch_shapes=[pltpu.VMEM((weight.shape[0] // BLOCK, weight.shape[1]), jnp.float32)],
        compiler_params=pltpu.CompilerParams(vmem_limit_bytes=14 * MIB),
        cost_estimate=pl.CostEstimate(flops=size * hint, bytes_accessed=2 * size * hint, transcendentals=0),
        name="prune",
    )(mask.T if turned else mask, weight)


def in_kernel(pruned, got_ref, *refs):
    share = got_ref.shape[2]
    if pruned:
        mask_ref, weight_ref, keep_ref, send_ref, lanes = refs
        count = weight_ref.shape[1] // share
    else:
        weight_hbm, keep_ref, send_ref, tiles, sems = refs
        count = tiles.shape[0]
        copies = [pltpu.make_async_copy(weight_hbm.at[n], tiles.at[n], sems.at[n]) for n in range(count)]
        for copy in copies:
            copy.start()
    if pruned:
        lanes[...] = jnp.dot(
            mask_ref[...].astype(jnp.bfloat16),
            pick_lanes(mask_ref.shape[1], lanes.shape[1]),
            preferred_element_type=jnp.float32,
        )
    core = lax.axis_index("wt") % 2
    x = jnp.concatenate(
        [
            got_ref[4 * place + 2 * chip + (core ^ other_core)].astype(jnp.float32)
            for place in range(4)
            for other_core in range(2)
            for chip in range(2)
        ],
        axis=0,
    ).astype(jnp.bfloat16)
    for n in range(count):
        cols = slice(n * share, (n + 1) * share)
        if not pruned:
            copies[n].wait()
            weight = tiles[n]
        else:
            weight = weight_ref[:, cols]
            weight = jnp.concatenate(
                [
                    weight[r * BLOCK : (r + 1) * BLOCK] * lanes[r : r + 1, cols].astype(jnp.bfloat16)
                    for r in range(lanes.shape[0])
                ],
                axis=0,
            )
        out = jnp.dot(x, weight, preferred_element_type=jnp.float32)
        keep_ref[:, cols] = jnp.concatenate([out[r : r + 8] for r in range(0, 64, 16)], axis=0)
        send_ref[:, cols] = jnp.concatenate([out[r + 8 : r + 16] for r in range(0, 64, 16)], axis=0).astype(jnp.bfloat16)


def in_products(got, weight, mask=None):
    places, count, depth = got.shape
    half, width = places * count // 2, weight.size // depth
    vmem = pl.BlockSpec(memory_space=pltpu.VMEM)
    if mask is None:
        scratch = [
            pltpu.VMEM((width // depth, depth, depth), jnp.bfloat16),
            pltpu.SemaphoreType.DMA((width // depth,)),
        ]
        given, places = [weight], [vmem, pl.BlockSpec(memory_space=pltpu.HBM)]
    else:
        scratch = [pltpu.VMEM((mask.shape[0], weight.shape[1]), jnp.float32)]
        given, places = [mask, weight], [vmem] * 3
    return pl.pallas_call(
        functools.partial(in_kernel, mask is not None),
        in_specs=places,
        out_shape=[
            jax.ShapeDtypeStruct((half, width), jnp.float32),
            jax.ShapeDtypeStruct((half, width), jnp.bfloat16),
        ],
        scratch_shapes=scratch,
        compiler_params=pltpu.CompilerParams(vmem_limit_bytes=(STREAM if mask is None else 14) * MIB),
        cost_estimate=pl.CostEstimate(flops=4 * half * weight.size, bytes_accessed=2 * weight.size, transcendentals=0),
        name="in_products",
    )(got, *given)


def share_kernel(kept_ref, got_ref, mine_ref, send_ref):
    total = kept_ref[...] + got_ref[...].astype(jnp.float32)
    rows = range(0, total.shape[0], 8)
    first = jnp.concatenate([total[r : r + 4] for r in rows], axis=0)
    second = jnp.concatenate([total[r + 4 : r + 8] for r in rows], axis=0)
    on_first = lax.axis_index("wt") < 2
    mine_ref[...] = jnp.where(on_first, first, second)
    send_ref[...] = jnp.where(on_first, second, first).astype(jnp.bfloat16)


def attend_kernel(images, part, own_ref, other_ref, bias_ref, gains_ref, out_ref):
    rows, share = out_ref.shape
    heads = share // HEAD

    def stacked(which):
        lanes = slice(which * share, (which + 1) * share)
        flat = own_ref[:, lanes] + other_ref[:, lanes].astype(jnp.float32)
        flat = (flat + bias_ref[which : which + 1, :]).astype(jnp.bfloat16)
        return jnp.concatenate([flat[:, h * HEAD : (h + 1) * HEAD] for h in range(heads)], axis=0)

    def normed(which):
        wide = stacked(which).astype(jnp.float32)
        scale = lax.rsqrt(jnp.mean(wide * wide, axis=-1, keepdims=True) + 1e-06)
        return (wide * scale * gains_ref[which : which + 1, :]).astype(jnp.bfloat16)

    queries, keys, values = normed(0), normed(1), stacked(2)
    scores = lax.dot_general(
        queries, keys, (((1,), (1,)), ((), ())), preferred_element_type=jnp.float32
    ) * (1.0 / math.sqrt(HEAD))
    size = heads * rows

    def group(dim):
        place = lax.broadcasted_iota(jnp.int32, (size, size), dim)
        return place // rows * images + place // part % images

    same = group(0) == group(1)
    weights = jnp.where(same, jnp.exp(jnp.where(same, scores, 0.0)), 0.0)
    denoms = jnp.sum(weights, axis=-1, keepdims=True)
    summed = jnp.dot(weights.astype(jnp.bfloat16), values, preferred_element_type=jnp.float32)
    attended = (summed / denoms).astype(jnp.bfloat16)
    for h in range(heads):
        out_ref[:, h * HEAD : (h + 1) * HEAD] = attended[h * rows : (h + 1) * rows]


def attention(images, part, own, other, bias, gains):
    return pl.pallas_call(
        functools.partial(attend_kernel, images, part),
        out_shape=jax.ShapeDtypeStruct((own.shape[0], bias.shape[1]), jnp.bfloat16),
        compiler_params=pltpu.CompilerParams(vmem_limit_bytes=8 * MIB),
        name="attention",
    )(own, other, bias, gains)


def hidden_kernel(own_ref, other_ref, bias_ref, out_ref):
    step = 6 * HEAD
    for start in range(0, out_ref.shape[1], step):
        lanes = slice(start, start + step)
        v = own_ref[:, lanes] + other_ref[:, lanes].astype(jnp.float32) + bias_ref[:, lanes]
        cubic = math.sqrt(2.0 / math.pi) * (v + 0.044715 * (v * v * v))
        out_ref[:, lanes] = (0.5 * v * (1.0 + jnp.tanh(cubic))).astype(jnp.bfloat16)


def activate(own, other, bias):
    return pl.pallas_call(
        hidden_kernel,
        out_shape=jax.ShapeDtypeStruct(own.shape, jnp.bfloat16),
        compiler_params=pltpu.CompilerParams(vmem_limit_bytes=8 * MIB),
        name="hidden",
    )(own, other, bias.reshape(1, -1))


def by_chip(mine, theirs):
    mine, theirs = mine.astype(jnp.float32), theirs.astype(jnp.float32)
    on_first = lax.axis_index("wt") < 2
    first, second = jnp.where(on_first, mine, theirs), jnp.where(on_first, theirs, mine)
    pieces = []
    for r in range(0, mine.shape[0], 4):
        pieces += [first[r : r + 4], second[r : r + 4]]
    return jnp.concatenate(pieces, axis=0).astype(jnp.bfloat16)


def out_kernel(a_mine, a_theirs, h_mine, h_theirs, proj_ref, down_ref, out_ref):
    half = a_mine.shape[0] // 2
    attended = jnp.concatenate([by_chip(ref[:half], ref[half:]) for ref in (a_mine, a_theirs)], axis=0)
    hidden = jnp.concatenate([h_mine[...], h_theirs[...]], axis=0)
    total = jnp.dot(attended, proj_ref[...], preferred_element_type=jnp.float32)
    total += jnp.dot(hidden, down_ref[...], preferred_element_type=jnp.float32)
    core = lax.axis_index("wt") % 2
    count = out_ref.shape[1]
    row = 0
    for other_core in range(2):
        for place in range(4):
            for chip in range(2):
                target = 4 * place + 2 * chip + (core ^ other_core)
                out_ref[target] = total[row : row + count].astype(out_ref.dtype)
                row += count


def out_products(count, attended, theirs, hidden, hidden_theirs, proj, down):
    rows, width = 2 * hidden.shape[0], proj.shape[1]
    size = proj.size + down.size
    return pl.pallas_call(
        out_kernel,
        out_shape=jax.ShapeDtypeStruct((rows // count, count, width), jnp.bfloat16),
        compiler_params=pltpu.CompilerParams(vmem_limit_bytes=12 * MIB),
        cost_estimate=pl.CostEstimate(flops=2 * rows * size, bytes_accessed=2 * size, transcendentals=0),
        name="out_products",
    )(attended, theirs, hidden, hidden_theirs, proj, down)


def swap(values, axis, bit):
    count = lax.axis_size(axis)
    return lax.ppermute(values, axis, [(i, i ^ bit) for i in range(count)])


def fixed_shards(
    tokens,
    modulation,
    qkv_weight,
    qkv_bias,
    norm_gains,
    up_weight,
    up_mask,
    up_bias,
    proj_weight,
    down_weight,
    down_mask,
    out_bias,
):
    count = tokens.shape[1]
    both = ("seq", "wt")
    got = lax.all_to_all(enter(tokens, modulation), both, split_axis=0, concat_axis=0, tiled=True)
    kept, given = in_products(got, qkv_weight.transpose(1, 0, 2))
    got, given = lax.optimization_barrier((got, given))
    half, width = kept.shape[0] // 2, kept.shape[1]
    halves = [jax.ShapeDtypeStruct((half, width), jnp.float32), jax.ShapeDtypeStruct((half, width), jnp.bfloat16)]
    own, sent = small(share_kernel, halves, kept, swap(given, "wt", 1))
    up_kept, up_given = in_products(got, up_weight, up_mask)
    up_given, sent = lax.optimization_barrier((up_given, sent))
    attended = attention(1, count, own, swap(sent, "wt", 2), qkv_bias, norm_gains)
    own = up_kept + swap(up_given, "wt", 1).astype(jnp.float32)
    pair = own, swap(own.astype(jnp.bfloat16), "wt", 2)
    down_pruned = prune(down_weight, down_mask, True, hint=0)
    attended = jnp.concatenate([attended, swap(attended, "wt", 2)], axis=0)
    attended, down_pruned = lax.optimization_barrier((attended, down_pruned))
    pair, attended = lax.optimization_barrier((pair, attended))
    hidden = activate(*pair, up_bias)
    shares = out_products(
        count, attended, swap(attended, "wt", 1), hidden, swap(hidden, "wt", 1), proj_weight, down_pruned
    )
    shares = lax.all_to_all(shares, both, split_axis=0, concat_axis=0, tiled=True)
    out = jax.ShapeDtypeStruct(tokens.shape, tokens.dtype)
    return small(leave_kernel, out, shares, tokens, modulation.transpose(1, 0, 2), out_bias.reshape(1, -1))


def solution(mesh):
    seq, wt = mesh.shape["seq"], mesh.shape["wt"]

    def shards(*args):
        share = args[2].shape[2]
        whole_heads = share % HEAD == 0 and share == args[8].shape[1] and args[5].shape[1] % share == 0
        fits = whole_heads and wt == 4 and seq == 4 and args[0].shape[1] == 4
        return (fixed_shards if fits else gathered_shards)(*args)

    return jax.shard_map(
        shards,
        mesh=mesh,
        in_specs=(
            P(("rep", "wt"), "seq", None),
            P(("rep", "wt"), None, None),
            P("wt", None, "seq"),
            P(None, "seq"),
            P(),
            P("wt", "seq"),
            P("wt", "seq"),
            P("seq"),
            P("seq", "wt"),
            P("seq", "wt"),
            P("seq", "wt"),
            P(),
        ),
        out_specs=P(("rep", "wt"), "seq", None),
        check_vma=False,
    )
```

```python
import functools
import math

import jax
import jax.numpy as jnp
from jax import lax
from jax.experimental import pallas as pl
from jax.experimental.pallas import tpu as pltpu
from jax.sharding import PartitionSpec as P

HEAD = 128
BLOCK = 64
MIB = 1024 * 1024
BESIDE = 16 * MIB


def masked(weight, keep_mask):
    row_blocks, col_blocks = keep_mask.shape
    expanded = jnp.broadcast_to(keep_mask[:, None, :, None], (row_blocks, BLOCK, col_blocks, BLOCK))
    return weight * expanded.reshape(weight.shape).astype(jnp.bfloat16)


def layer_norm(values):
    center = values - jnp.mean(values, axis=-1, keepdims=True)
    spread = jnp.mean(center * center, axis=-1, keepdims=True)
    return center * lax.rsqrt(spread + 1e-06)


def norm_heads(flat_rows, gains):
    shaped_rows = flat_rows.reshape(flat_rows.shape[0], -1, HEAD).astype(jnp.float32)
    scaled = (
        shaped_rows
        * lax.rsqrt(jnp.mean(shaped_rows * shaped_rows, axis=-1, keepdims=True) + 1e-06)
        * gains
    )
    return scaled.astype(jnp.bfloat16)


def attend(queries, keys_normed, values):
    scores = jnp.einsum(
        "qhd,khd->hqk", queries, keys_normed, preferred_element_type=jnp.float32
    ) / math.sqrt(HEAD)
    weights = jnp.exp(scores)
    denoms = jnp.sum(weights, axis=2)
    summed = jnp.einsum(
        "hqk,khd->qhd", weights.astype(jnp.bfloat16), values, preferred_element_type=jnp.float32
    )
    return (summed, denoms)


def gathered_shards(
    tokens,
    modulation,
    qkv_weight,
    qkv_bias,
    norm_gains,
    up_weight,
    up_mask,
    up_bias,
    proj_weight,
    down_weight,
    down_mask,
    out_bias,
):
    own_rows = tokens[0]
    mod_rows = modulation[0]
    row_count = own_rows.shape[0]
    feature_count = own_rows.shape[1]
    head_count = feature_count // HEAD
    normed = layer_norm(own_rows.astype(jnp.float32))
    shaped = ((1.0 + mod_rows[1]) * normed + mod_rows[0]).astype(jnp.bfloat16)
    gathered = lax.all_gather(shaped, "seq", axis=0, tiled=True)
    seq_len = gathered.shape[0]
    col_share = qkv_weight.shape[2]
    up_local = masked(up_weight, up_mask)
    pieces = (
        lax.all_gather(qkv_weight, "wt", axis=0, tiled=True),
        lax.all_gather(up_local, "wt", axis=0, tiled=True),
    )
    piece_rows = pieces[0].shape[0]
    first = jnp.dot(
        gathered, pieces[0].reshape(piece_rows, 3 * col_share), preferred_element_type=jnp.float32
    )
    second = jnp.dot(gathered, pieces[1], preferred_element_type=jnp.float32)
    qkv_local = (first.reshape(seq_len, 3, col_share) + qkv_bias).astype(jnp.bfloat16)
    hidden = jax.nn.gelu(second + up_bias, approximate=True).astype(jnp.bfloat16)
    query_flat = lax.all_to_all(qkv_local[:, 0, :], "seq", split_axis=0, concat_axis=1, tiled=True)
    kv_whole = lax.all_gather(qkv_local[:, 1:, :], "seq", axis=2, tiled=True)
    queries = norm_heads(query_flat, norm_gains[0])
    keys_normed = norm_heads(kv_whole[:, 0, :], norm_gains[1])
    values = kv_whole[:, 1, :].reshape(seq_len, head_count, HEAD)
    summed, denoms = attend(queries, keys_normed, values)
    attended = (
        (summed / denoms.T[:, :, None]).reshape(row_count, feature_count).astype(jnp.bfloat16)
    )
    attended_cols = lax.all_to_all(attended, "seq", split_axis=1, concat_axis=0, tiled=True)
    down_local = masked(down_weight, down_mask)
    proj_full, down_full = (
        lax.all_gather(proj_weight, "wt", axis=1, tiled=True),
        lax.all_gather(down_local, "wt", axis=1, tiled=True),
    )
    branch_sum = lax.psum_scatter(
        jnp.dot(attended_cols, proj_full, preferred_element_type=jnp.float32)
        + jnp.dot(hidden, down_full, preferred_element_type=jnp.float32),
        "seq",
        scatter_dimension=0,
        tiled=True,
    )
    result = own_rows.astype(jnp.float32) + mod_rows[2] * (branch_sum + out_bias)
    return result.astype(jnp.bfloat16)[None]


def enter_kernel(tokens_ref, mod_ref, out_ref):
    shaped = (1.0 + mod_ref[1]) * layer_norm(tokens_ref[0].astype(jnp.float32)) + mod_ref[0]
    shaped = shaped.astype(jnp.bfloat16)
    share = out_ref.shape[2]
    for place in range(out_ref.shape[0]):
        out_ref[place] = shaped[:, place % 4 * share : (place % 4 + 1) * share]


def enter(tokens, modulation):
    _, count, features = tokens.shape
    return pl.pallas_call(
        enter_kernel,
        out_shape=jax.ShapeDtypeStruct((16, count, features // 4), jnp.bfloat16),
        compiler_params=pltpu.CompilerParams(vmem_limit_bytes=4 * MIB),
        cost_estimate=pl.CostEstimate(flops=400 * BESIDE, bytes_accessed=BESIDE, transcendentals=BESIDE // 100),
        name="enter",
    )(tokens, modulation.transpose(1, 0, 2))


def leave_kernel(shares_ref, tokens_ref, mod_ref, bias_ref, out_ref):
    share = shares_ref.shape[2]
    for n in range(4):
        lanes = slice(n * share, (n + 1) * share)
        branch = sum(shares_ref[4 * place + n].astype(jnp.float32) for place in range(4)) + bias_ref[:, lanes]
        out_ref[0, :, lanes] = (tokens_ref[0, :, lanes].astype(jnp.float32) + mod_ref[2, :, lanes] * branch).astype(out_ref.dtype)


def small(kernel, outs, *args):
    return pl.pallas_call(
        kernel,
        out_shape=outs,
        compiler_params=pltpu.CompilerParams(vmem_limit_bytes=4 * MIB),
        name=kernel.__name__,
    )(*args)


def pick_lanes(blocks, lanes):
    return (
        lax.broadcasted_iota(jnp.int32, (blocks, lanes), 1) // BLOCK
        == lax.broadcasted_iota(jnp.int32, (blocks, lanes), 0)
    ).astype(jnp.bfloat16)


def prune_kernel(mask_dim, mask_ref, weight_ref, out_ref, lanes):
    lanes[...] = lax.dot_general(
        mask_ref[...].astype(jnp.bfloat16),
        pick_lanes(mask_ref.shape[mask_dim], out_ref.shape[1]),
        (((mask_dim,), (0,)), ((), ())),
        preferred_element_type=jnp.float32,
    )

    def body(b, _):
        rows = pl.ds(pl.multiple_of(b * BLOCK, BLOCK), BLOCK)
        out_ref[rows, :] = weight_ref[rows, :] * lanes[pl.ds(b, 1), :].astype(jnp.bfloat16)
        return 0

    lax.fori_loop(0, out_ref.shape[0] // BLOCK, body, 0)


def prune(weight, mask, turned, hint=1):
    size = 2 * weight.size
    return pl.pallas_call(
        functools.partial(prune_kernel, 0 if turned else 1),
        out_shape=jax.ShapeDtypeStruct(weight.shape, jnp.bfloat16),
        scratch_shapes=[pltpu.VMEM((weight.shape[0] // BLOCK, weight.shape[1]), jnp.float32)],
        compiler_params=pltpu.CompilerParams(vmem_limit_bytes=14 * MIB),
        cost_estimate=pl.CostEstimate(flops=size * hint, bytes_accessed=2 * size * hint, transcendentals=0),
        name="prune",
    )(mask.T if turned else mask, weight)


def in_kernel(pruned, got_ref, *refs):
    share = got_ref.shape[2]
    if pruned:
        mask_ref, weight_ref, keep_ref, send_ref, lanes = refs
        lanes[...] = jnp.dot(
            mask_ref[...].astype(jnp.bfloat16),
            pick_lanes(mask_ref.shape[1], lanes.shape[1]),
            preferred_element_type=jnp.float32,
        )
    else:
        weight_ref, keep_ref, send_ref = refs
    core = lax.axis_index("wt") % 2
    x = jnp.concatenate(
        [
            got_ref[4 * place + 2 * chip + (core ^ other_core)].astype(jnp.float32)
            for place in range(4)
            for other_core in range(2)
            for chip in range(2)
        ],
        axis=0,
    ).astype(jnp.bfloat16)
    for n in range(keep_ref.shape[1] // share):
        cols = slice(n * share, (n + 1) * share)
        if pruned:
            weight = jnp.concatenate(
                [
                    weight_ref[r * BLOCK : (r + 1) * BLOCK, cols] * lanes[r : r + 1, cols].astype(jnp.bfloat16)
                    for r in range(lanes.shape[0])
                ],
                axis=0,
            )
        else:
            weight = weight_ref[n]
        out = jnp.dot(x, weight, preferred_element_type=jnp.float32)
        keep_ref[:, cols] = jnp.concatenate([out[r : r + 8] for r in range(0, 64, 16)], axis=0)
        send_ref[:, cols] = jnp.concatenate([out[r + 8 : r + 16] for r in range(0, 64, 16)], axis=0).astype(jnp.bfloat16)


def in_products(got, weight, mask=None):
    places, count, depth = got.shape
    half, width = places * count // 2, weight.size // depth
    pruned = mask is not None
    return pl.pallas_call(
        functools.partial(in_kernel, pruned),
        out_shape=[
            jax.ShapeDtypeStruct((half, width), jnp.float32),
            jax.ShapeDtypeStruct((half, width), jnp.bfloat16),
        ],
        scratch_shapes=[pltpu.VMEM((mask.shape[0], weight.shape[1]), jnp.float32)] if pruned else [],
        compiler_params=pltpu.CompilerParams(vmem_limit_bytes=14 * MIB),
        cost_estimate=pl.CostEstimate(flops=4 * half * weight.size, bytes_accessed=2 * weight.size, transcendentals=0),
        name="in_products",
    )(got, *([mask] if pruned else []), weight)


def share_kernel(kept_ref, got_ref, mine_ref, send_ref):
    total = kept_ref[...] + got_ref[...].astype(jnp.float32)
    rows = range(0, total.shape[0], 8)
    first = jnp.concatenate([total[r : r + 4] for r in rows], axis=0)
    second = jnp.concatenate([total[r + 4 : r + 8] for r in rows], axis=0)
    on_first = lax.axis_index("wt") < 2
    mine_ref[...] = jnp.where(on_first, first, second)
    send_ref[...] = jnp.where(on_first, second, first).astype(jnp.bfloat16)


def attend_kernel(images, part, own_ref, other_ref, bias_ref, gains_ref, out_ref):
    rows, share = out_ref.shape
    heads = share // HEAD

    def stacked(which):
        lanes = slice(which * share, (which + 1) * share)
        flat = own_ref[:, lanes] + other_ref[:, lanes].astype(jnp.float32)
        flat = (flat + bias_ref[which : which + 1, :]).astype(jnp.bfloat16)
        return jnp.concatenate([flat[:, h * HEAD : (h + 1) * HEAD] for h in range(heads)], axis=0)

    def normed(which):
        wide = stacked(which).astype(jnp.float32)
        scale = lax.rsqrt(jnp.mean(wide * wide, axis=-1, keepdims=True) + 1e-06)
        return (wide * scale * gains_ref[which : which + 1, :]).astype(jnp.bfloat16)

    queries, keys, values = normed(0), normed(1), stacked(2)
    scores = lax.dot_general(
        queries, keys, (((1,), (1,)), ((), ())), preferred_element_type=jnp.float32
    ) * (1.0 / math.sqrt(HEAD))
    size = heads * rows

    def group(dim):
        place = lax.broadcasted_iota(jnp.int32, (size, size), dim)
        return place // rows * images + place // part % images

    same = group(0) == group(1)
    weights = jnp.where(same, jnp.exp(jnp.where(same, scores, 0.0)), 0.0)
    denoms = jnp.sum(weights, axis=-1, keepdims=True)
    summed = jnp.dot(weights.astype(jnp.bfloat16), values, preferred_element_type=jnp.float32)
    attended = (summed / denoms).astype(jnp.bfloat16)
    for h in range(heads):
        out_ref[:, h * HEAD : (h + 1) * HEAD] = attended[h * rows : (h + 1) * rows]


def attention(images, part, own, other, bias, gains):
    return pl.pallas_call(
        functools.partial(attend_kernel, images, part),
        out_shape=jax.ShapeDtypeStruct((own.shape[0], bias.shape[1]), jnp.bfloat16),
        compiler_params=pltpu.CompilerParams(vmem_limit_bytes=8 * MIB),
        name="attention",
    )(own, other, bias, gains)


def hidden_kernel(own_ref, other_ref, bias_ref, out_ref):
    step = 6 * HEAD
    for start in range(0, out_ref.shape[1], step):
        lanes = slice(start, start + step)
        v = own_ref[:, lanes] + other_ref[:, lanes].astype(jnp.float32) + bias_ref[:, lanes]
        cubic = math.sqrt(2.0 / math.pi) * (v + 0.044715 * (v * v * v))
        out_ref[:, lanes] = (0.5 * v * (1.0 + jnp.tanh(cubic))).astype(jnp.bfloat16)


def activate(own, other, bias):
    return pl.pallas_call(
        hidden_kernel,
        out_shape=jax.ShapeDtypeStruct(own.shape, jnp.bfloat16),
        compiler_params=pltpu.CompilerParams(vmem_limit_bytes=8 * MIB),
        name="hidden",
    )(own, other, bias.reshape(1, -1))


def by_chip(mine, theirs):
    mine, theirs = mine.astype(jnp.float32), theirs.astype(jnp.float32)
    on_first = lax.axis_index("wt") < 2
    first, second = jnp.where(on_first, mine, theirs), jnp.where(on_first, theirs, mine)
    pieces = []
    for r in range(0, mine.shape[0], 4):
        pieces += [first[r : r + 4], second[r : r + 4]]
    return jnp.concatenate(pieces, axis=0).astype(jnp.bfloat16)


def out_kernel(a_mine, a_theirs, h_mine, h_theirs, proj_ref, down_ref, out_ref):
    half = a_mine.shape[0] // 2
    attended = jnp.concatenate([by_chip(ref[:half], ref[half:]) for ref in (a_mine, a_theirs)], axis=0)
    hidden = jnp.concatenate([h_mine[...], h_theirs[...]], axis=0)
    total = jnp.dot(attended, proj_ref[...], preferred_element_type=jnp.float32)
    total += jnp.dot(hidden, down_ref[...], preferred_element_type=jnp.float32)
    core = lax.axis_index("wt") % 2
    count = out_ref.shape[1]
    row = 0
    for other_core in range(2):
        for place in range(4):
            for chip in range(2):
                target = 4 * place + 2 * chip + (core ^ other_core)
                out_ref[target] = total[row : row + count].astype(out_ref.dtype)
                row += count


def out_products(count, attended, theirs, hidden, hidden_theirs, proj, down):
    rows, width = 2 * hidden.shape[0], proj.shape[1]
    size = proj.size + down.size
    return pl.pallas_call(
        out_kernel,
        out_shape=jax.ShapeDtypeStruct((rows // count, count, width), jnp.bfloat16),
        compiler_params=pltpu.CompilerParams(vmem_limit_bytes=12 * MIB),
        cost_estimate=pl.CostEstimate(flops=2 * rows * size, bytes_accessed=2 * size, transcendentals=0),
        name="out_products",
    )(attended, theirs, hidden, hidden_theirs, proj, down)


def swap(values, axis, bit):
    count = lax.axis_size(axis)
    return lax.ppermute(values, axis, [(i, i ^ bit) for i in range(count)])


def fixed_shards(
    tokens,
    modulation,
    qkv_weight,
    qkv_bias,
    norm_gains,
    up_weight,
    up_mask,
    up_bias,
    proj_weight,
    down_weight,
    down_mask,
    out_bias,
):
    count = tokens.shape[1]
    both = ("seq", "wt")
    got = lax.all_to_all(enter(tokens, modulation), both, split_axis=0, concat_axis=0, tiled=True)
    kept, given = in_products(got, qkv_weight.transpose(1, 0, 2))
    got, given = lax.optimization_barrier((got, given))
    half, width = kept.shape[0] // 2, kept.shape[1]
    halves = [jax.ShapeDtypeStruct((half, width), jnp.float32), jax.ShapeDtypeStruct((half, width), jnp.bfloat16)]
    own, sent = small(share_kernel, halves, kept, swap(given, "wt", 1))
    up_kept, up_given = in_products(got, up_weight, up_mask)
    up_given, sent = lax.optimization_barrier((up_given, sent))
    attended = attention(1, count, own, swap(sent, "wt", 2), qkv_bias, norm_gains)
    own = up_kept + swap(up_given, "wt", 1).astype(jnp.float32)
    pair = own, swap(own.astype(jnp.bfloat16), "wt", 2)
    down_pruned = prune(down_weight, down_mask, True, hint=0)
    attended = jnp.concatenate([attended, swap(attended, "wt", 2)], axis=0)
    attended, down_pruned = lax.optimization_barrier((attended, down_pruned))
    pair, attended = lax.optimization_barrier((pair, attended))
    hidden = activate(*pair, up_bias)
    shares = out_products(
        count, attended, swap(attended, "wt", 1), hidden, swap(hidden, "wt", 1), proj_weight, down_pruned
    )
    shares = lax.all_to_all(shares, both, split_axis=0, concat_axis=0, tiled=True)
    out = jax.ShapeDtypeStruct(tokens.shape, tokens.dtype)
    return small(leave_kernel, out, shares, tokens, modulation.transpose(1, 0, 2), out_bias.reshape(1, -1))


def solution(mesh):
    seq, wt = mesh.shape["seq"], mesh.shape["wt"]

    def shards(*args):
        share = args[2].shape[2]
        whole_heads = share % HEAD == 0 and share == args[8].shape[1] and args[5].shape[1] % share == 0
        fits = whole_heads and wt == 4 and seq == 4 and args[0].shape[1] == 4
        return (fixed_shards if fits else gathered_shards)(*args)

    return jax.shard_map(
        shards,
        mesh=mesh,
        in_specs=(
            P(("rep", "wt"), "seq", None),
            P(("rep", "wt"), None, None),
            P("wt", None, "seq"),
            P(None, "seq"),
            P(),
            P("wt", "seq"),
            P("wt", "seq"),
            P("seq"),
            P("seq", "wt"),
            P("seq", "wt"),
            P("seq", "wt"),
            P(),
        ),
        out_specs=P(("rep", "wt"), "seq", None),
        check_vma=False,
    )
```

```python
import functools
import math

import jax
import jax.numpy as jnp
from jax import lax
from jax.experimental import pallas as pl
from jax.experimental.pallas import tpu as pltpu
from jax.sharding import PartitionSpec as P

HEAD = 128
BLOCK = 64
MIB = 1024 * 1024
BESIDE = 16 * MIB


def masked(weight, keep_mask):
    row_blocks, col_blocks = keep_mask.shape
    expanded = jnp.broadcast_to(keep_mask[:, None, :, None], (row_blocks, BLOCK, col_blocks, BLOCK))
    return weight * expanded.reshape(weight.shape).astype(jnp.bfloat16)


def layer_norm(values):
    center = values - jnp.mean(values, axis=-1, keepdims=True)
    spread = jnp.mean(center * center, axis=-1, keepdims=True)
    return center * lax.rsqrt(spread + 1e-06)


def norm_heads(flat_rows, gains):
    shaped_rows = flat_rows.reshape(flat_rows.shape[0], -1, HEAD).astype(jnp.float32)
    scaled = (
        shaped_rows
        * lax.rsqrt(jnp.mean(shaped_rows * shaped_rows, axis=-1, keepdims=True) + 1e-06)
        * gains
    )
    return scaled.astype(jnp.bfloat16)


def attend(queries, keys_normed, values):
    scores = jnp.einsum(
        "qhd,khd->hqk", queries, keys_normed, preferred_element_type=jnp.float32
    ) / math.sqrt(HEAD)
    weights = jnp.exp(scores)
    denoms = jnp.sum(weights, axis=2)
    summed = jnp.einsum(
        "hqk,khd->qhd", weights.astype(jnp.bfloat16), values, preferred_element_type=jnp.float32
    )
    return (summed, denoms)


def gathered_shards(
    tokens,
    modulation,
    qkv_weight,
    qkv_bias,
    norm_gains,
    up_weight,
    up_mask,
    up_bias,
    proj_weight,
    down_weight,
    down_mask,
    out_bias,
):
    own_rows = tokens[0]
    mod_rows = modulation[0]
    row_count = own_rows.shape[0]
    feature_count = own_rows.shape[1]
    head_count = feature_count // HEAD
    normed = layer_norm(own_rows.astype(jnp.float32))
    shaped = ((1.0 + mod_rows[1]) * normed + mod_rows[0]).astype(jnp.bfloat16)
    gathered = lax.all_gather(shaped, "seq", axis=0, tiled=True)
    seq_len = gathered.shape[0]
    col_share = qkv_weight.shape[2]
    up_local = masked(up_weight, up_mask)
    pieces = (
        lax.all_gather(qkv_weight, "wt", axis=0, tiled=True),
        lax.all_gather(up_local, "wt", axis=0, tiled=True),
    )
    piece_rows = pieces[0].shape[0]
    first = jnp.dot(
        gathered, pieces[0].reshape(piece_rows, 3 * col_share), preferred_element_type=jnp.float32
    )
    second = jnp.dot(gathered, pieces[1], preferred_element_type=jnp.float32)
    qkv_local = (first.reshape(seq_len, 3, col_share) + qkv_bias).astype(jnp.bfloat16)
    hidden = jax.nn.gelu(second + up_bias, approximate=True).astype(jnp.bfloat16)
    query_flat = lax.all_to_all(qkv_local[:, 0, :], "seq", split_axis=0, concat_axis=1, tiled=True)
    kv_whole = lax.all_gather(qkv_local[:, 1:, :], "seq", axis=2, tiled=True)
    queries = norm_heads(query_flat, norm_gains[0])
    keys_normed = norm_heads(kv_whole[:, 0, :], norm_gains[1])
    values = kv_whole[:, 1, :].reshape(seq_len, head_count, HEAD)
    summed, denoms = attend(queries, keys_normed, values)
    attended = (
        (summed / denoms.T[:, :, None]).reshape(row_count, feature_count).astype(jnp.bfloat16)
    )
    attended_cols = lax.all_to_all(attended, "seq", split_axis=1, concat_axis=0, tiled=True)
    down_local = masked(down_weight, down_mask)
    proj_full, down_full = (
        lax.all_gather(proj_weight, "wt", axis=1, tiled=True),
        lax.all_gather(down_local, "wt", axis=1, tiled=True),
    )
    branch_sum = lax.psum_scatter(
        jnp.dot(attended_cols, proj_full, preferred_element_type=jnp.float32)
        + jnp.dot(hidden, down_full, preferred_element_type=jnp.float32),
        "seq",
        scatter_dimension=0,
        tiled=True,
    )
    result = own_rows.astype(jnp.float32) + mod_rows[2] * (branch_sum + out_bias)
    return result.astype(jnp.bfloat16)[None]


def enter_kernel(tokens_ref, mod_ref, mask_ref, pick_ref, out_ref, lanes_ref):
    lanes_ref[...] = jnp.dot(mask_ref[...].astype(jnp.bfloat16), pick_ref[...], preferred_element_type=jnp.float32)
    shaped = (1.0 + mod_ref[1]) * layer_norm(tokens_ref[0].astype(jnp.float32)) + mod_ref[0]
    shaped = shaped.astype(jnp.bfloat16)
    share = out_ref.shape[2]
    for place in range(out_ref.shape[0]):
        out_ref[place] = shaped[:, place % 4 * share : (place % 4 + 1) * share]


def enter(tokens, modulation, mask, pick):
    _, count, features = tokens.shape
    return pl.pallas_call(
        enter_kernel,
        out_shape=[
            jax.ShapeDtypeStruct((16, count, features // 4), jnp.bfloat16),
            jax.ShapeDtypeStruct((mask.shape[0], pick.shape[1]), jnp.float32),
        ],
        compiler_params=pltpu.CompilerParams(vmem_limit_bytes=4 * MIB),
        cost_estimate=pl.CostEstimate(flops=400 * BESIDE, bytes_accessed=BESIDE, transcendentals=BESIDE // 100),
        name="enter",
    )(tokens, modulation.transpose(1, 0, 2), mask, pick)


def leave_kernel(shares_ref, tokens_ref, mod_ref, bias_ref, out_ref):
    share = shares_ref.shape[2]
    for n in range(4):
        lanes = slice(n * share, (n + 1) * share)
        branch = sum(shares_ref[4 * place + n].astype(jnp.float32) for place in range(4)) + bias_ref[:, lanes]
        out_ref[0, :, lanes] = (tokens_ref[0, :, lanes].astype(jnp.float32) + mod_ref[2, :, lanes] * branch).astype(out_ref.dtype)


def small(kernel, outs, *args):
    return pl.pallas_call(
        kernel,
        out_shape=outs,
        compiler_params=pltpu.CompilerParams(vmem_limit_bytes=4 * MIB),
        name=kernel.__name__,
    )(*args)


def pick_lanes(blocks, lanes):
    return (
        lax.broadcasted_iota(jnp.int32, (blocks, lanes), 1) // BLOCK
        == lax.broadcasted_iota(jnp.int32, (blocks, lanes), 0)
    ).astype(jnp.bfloat16)


def pick_kernel(out_ref):
    out_ref[...] = pick_lanes(*out_ref.shape)


def picks(blocks, lanes):
    return pl.pallas_call(
        pick_kernel,
        out_shape=jax.ShapeDtypeStruct((blocks, lanes), jnp.bfloat16),
        compiler_params=pltpu.CompilerParams(vmem_limit_bytes=4 * MIB),
        cost_estimate=pl.CostEstimate(flops=400 * BESIDE, bytes_accessed=BESIDE, transcendentals=BESIDE // 100),
        name="picks",
    )()


def prune_kernel(mask_dim, mask_ref, weight_ref, out_ref, lanes):
    lanes[...] = lax.dot_general(
        mask_ref[...].astype(jnp.bfloat16),
        pick_lanes(mask_ref.shape[mask_dim], out_ref.shape[1]),
        (((mask_dim,), (0,)), ((), ())),
        preferred_element_type=jnp.float32,
    )

    def body(b, _):
        rows = pl.ds(pl.multiple_of(b * BLOCK, BLOCK), BLOCK)
        out_ref[rows, :] = weight_ref[rows, :] * lanes[pl.ds(b, 1), :].astype(jnp.bfloat16)
        return 0

    lax.fori_loop(0, out_ref.shape[0] // BLOCK, body, 0)


def prune(weight, mask, turned, hint=1):
    size = 2 * weight.size
    return pl.pallas_call(
        functools.partial(prune_kernel, 0 if turned else 1),
        out_shape=jax.ShapeDtypeStruct(weight.shape, jnp.bfloat16),
        scratch_shapes=[pltpu.VMEM((weight.shape[0] // BLOCK, weight.shape[1]), jnp.float32)],
        compiler_params=pltpu.CompilerParams(vmem_limit_bytes=14 * MIB),
        cost_estimate=pl.CostEstimate(flops=size * hint, bytes_accessed=2 * size * hint, transcendentals=0),
        name="prune",
    )(mask.T if turned else mask, weight)


def in_kernel(pruned, got_ref, *refs):
    share = got_ref.shape[2]
    if pruned:
        lanes, weight_ref, keep_ref, send_ref = refs
    else:
        weight_ref, keep_ref, send_ref = refs
    core = lax.axis_index("wt") % 2
    x = jnp.concatenate(
        [
            got_ref[4 * place + 2 * chip + (core ^ other_core)].astype(jnp.float32)
            for place in range(4)
            for other_core in range(2)
            for chip in range(2)
        ],
        axis=0,
    ).astype(jnp.bfloat16)
    for n in range(keep_ref.shape[1] // share):
        cols = slice(n * share, (n + 1) * share)
        if pruned:
            weight = jnp.concatenate(
                [
                    weight_ref[r * BLOCK : (r + 1) * BLOCK, cols] * lanes[r : r + 1, cols].astype(jnp.bfloat16)
                    for r in range(lanes.shape[0])
                ],
                axis=0,
            )
        else:
            weight = weight_ref[n]
        out = jnp.dot(x, weight, preferred_element_type=jnp.float32)
        keep_ref[:, cols] = jnp.concatenate([out[r : r + 8] for r in range(0, 64, 16)], axis=0)
        send_ref[:, cols] = jnp.concatenate([out[r + 8 : r + 16] for r in range(0, 64, 16)], axis=0).astype(jnp.bfloat16)


def in_products(got, weight, lanes=None):
    places, count, depth = got.shape
    half, width = places * count // 2, weight.size // depth
    pruned = lanes is not None
    return pl.pallas_call(
        functools.partial(in_kernel, pruned),
        out_shape=[
            jax.ShapeDtypeStruct((half, width), jnp.float32),
            jax.ShapeDtypeStruct((half, width), jnp.bfloat16),
        ],
        compiler_params=pltpu.CompilerParams(vmem_limit_bytes=14 * MIB),
        cost_estimate=pl.CostEstimate(flops=4 * half * weight.size, bytes_accessed=2 * weight.size, transcendentals=0),
        name="in_products",
    )(got, *([lanes] if pruned else []), weight)


def share_kernel(kept_ref, got_ref, mine_ref, send_ref):
    total = kept_ref[...] + got_ref[...].astype(jnp.float32)
    rows = range(0, total.shape[0], 8)
    first = jnp.concatenate([total[r : r + 4] for r in rows], axis=0)
    second = jnp.concatenate([total[r + 4 : r + 8] for r in rows], axis=0)
    on_first = lax.axis_index("wt") < 2
    mine_ref[...] = jnp.where(on_first, first, second)
    send_ref[...] = jnp.where(on_first, second, first).astype(jnp.bfloat16)


def attend_kernel(images, part, own_ref, other_ref, bias_ref, gains_ref, out_ref):
    rows, share = out_ref.shape
    heads = share // HEAD

    def stacked(which):
        lanes = slice(which * share, (which + 1) * share)
        flat = own_ref[:, lanes] + other_ref[:, lanes].astype(jnp.float32)
        flat = (flat + bias_ref[which : which + 1, :]).astype(jnp.bfloat16)
        return jnp.concatenate([flat[:, h * HEAD : (h + 1) * HEAD] for h in range(heads)], axis=0)

    def normed(which):
        wide = stacked(which).astype(jnp.float32)
        scale = lax.rsqrt(jnp.mean(wide * wide, axis=-1, keepdims=True) + 1e-06)
        return (wide * scale * gains_ref[which : which + 1, :]).astype(jnp.bfloat16)

    queries, keys, values = normed(0), normed(1), stacked(2)
    scores = lax.dot_general(
        queries, keys, (((1,), (1,)), ((), ())), preferred_element_type=jnp.float32
    ) * (1.0 / math.sqrt(HEAD))
    size = heads * rows

    def group(dim):
        place = lax.broadcasted_iota(jnp.int32, (size, size), dim)
        return place // rows * images + place // part % images

    same = group(0) == group(1)
    weights = jnp.where(same, jnp.exp(jnp.where(same, scores, 0.0)), 0.0)
    denoms = jnp.sum(weights, axis=-1, keepdims=True)
    summed = jnp.dot(weights.astype(jnp.bfloat16), values, preferred_element_type=jnp.float32)
    attended = (summed / denoms).astype(jnp.bfloat16)
    for h in range(heads):
        out_ref[:, h * HEAD : (h + 1) * HEAD] = attended[h * rows : (h + 1) * rows]


def attention(images, part, own, other, bias, gains):
    return pl.pallas_call(
        functools.partial(attend_kernel, images, part),
        out_shape=jax.ShapeDtypeStruct((own.shape[0], bias.shape[1]), jnp.bfloat16),
        compiler_params=pltpu.CompilerParams(vmem_limit_bytes=8 * MIB),
        name="attention",
    )(own, other, bias, gains)


def hidden_kernel(own_ref, other_ref, bias_ref, out_ref):
    step = 6 * HEAD
    for start in range(0, out_ref.shape[1], step):
        lanes = slice(start, start + step)
        v = own_ref[:, lanes] + other_ref[:, lanes].astype(jnp.float32) + bias_ref[:, lanes]
        cubic = math.sqrt(2.0 / math.pi) * (v + 0.044715 * (v * v * v))
        out_ref[:, lanes] = (0.5 * v * (1.0 + jnp.tanh(cubic))).astype(jnp.bfloat16)


def activate(own, other, bias):
    return pl.pallas_call(
        hidden_kernel,
        out_shape=jax.ShapeDtypeStruct(own.shape, jnp.bfloat16),
        compiler_params=pltpu.CompilerParams(vmem_limit_bytes=8 * MIB),
        name="hidden",
    )(own, other, bias.reshape(1, -1))


def by_chip(mine, theirs):
    mine, theirs = mine.astype(jnp.float32), theirs.astype(jnp.float32)
    on_first = lax.axis_index("wt") < 2
    first, second = jnp.where(on_first, mine, theirs), jnp.where(on_first, theirs, mine)
    pieces = []
    for r in range(0, mine.shape[0], 4):
        pieces += [first[r : r + 4], second[r : r + 4]]
    return jnp.concatenate(pieces, axis=0).astype(jnp.bfloat16)


def out_kernel(a_mine, a_theirs, h_mine, h_theirs, proj_ref, down_ref, out_ref):
    half = a_mine.shape[0] // 2
    attended = jnp.concatenate([by_chip(ref[:half], ref[half:]) for ref in (a_mine, a_theirs)], axis=0)
    hidden = jnp.concatenate([h_mine[...], h_theirs[...]], axis=0)
    total = jnp.dot(attended, proj_ref[...], preferred_element_type=jnp.float32)
    total += jnp.dot(hidden, down_ref[...], preferred_element_type=jnp.float32)
    core = lax.axis_index("wt") % 2
    count = out_ref.shape[1]
    row = 0
    for other_core in range(2):
        for place in range(4):
            for chip in range(2):
                target = 4 * place + 2 * chip + (core ^ other_core)
                out_ref[target] = total[row : row + count].astype(out_ref.dtype)
                row += count


def out_products(count, attended, theirs, hidden, hidden_theirs, proj, down):
    rows, width = 2 * hidden.shape[0], proj.shape[1]
    size = proj.size + down.size
    return pl.pallas_call(
        out_kernel,
        out_shape=jax.ShapeDtypeStruct((rows // count, count, width), jnp.bfloat16),
        compiler_params=pltpu.CompilerParams(vmem_limit_bytes=12 * MIB),
        cost_estimate=pl.CostEstimate(flops=2 * rows * size, bytes_accessed=2 * size, transcendentals=0),
        name="out_products",
    )(attended, theirs, hidden, hidden_theirs, proj, down)


def swap(values, axis, bit):
    count = lax.axis_size(axis)
    return lax.ppermute(values, axis, [(i, i ^ bit) for i in range(count)])


def fixed_shards(
    tokens,
    modulation,
    qkv_weight,
    qkv_bias,
    norm_gains,
    up_weight,
    up_mask,
    up_bias,
    proj_weight,
    down_weight,
    down_mask,
    out_bias,
):
    count = tokens.shape[1]
    both = ("seq", "wt")
    sent, lanes = enter(tokens, modulation, up_mask, picks(up_mask.shape[1], up_weight.shape[1]))
    got = lax.all_to_all(sent, both, split_axis=0, concat_axis=0, tiled=True)
    kept, given = in_products(got, qkv_weight.transpose(1, 0, 2))
    got, given = lax.optimization_barrier((got, given))
    half, width = kept.shape[0] // 2, kept.shape[1]
    halves = [jax.ShapeDtypeStruct((half, width), jnp.float32), jax.ShapeDtypeStruct((half, width), jnp.bfloat16)]
    own, sent = small(share_kernel, halves, kept, swap(given, "wt", 1))
    up_kept, up_given = in_products(got, up_weight, lanes)
    up_given, sent = lax.optimization_barrier((up_given, sent))
    attended = attention(1, count, own, swap(sent, "wt", 2), qkv_bias, norm_gains)
    own = up_kept + swap(up_given, "wt", 1).astype(jnp.float32)
    pair = own, swap(own.astype(jnp.bfloat16), "wt", 2)
    down_pruned = prune(down_weight, down_mask, True, hint=0)
    attended = jnp.concatenate([attended, swap(attended, "wt", 2)], axis=0)
    attended, down_pruned = lax.optimization_barrier((attended, down_pruned))
    pair, attended = lax.optimization_barrier((pair, attended))
    hidden = activate(*pair, up_bias)
    shares = out_products(
        count, attended, swap(attended, "wt", 1), hidden, swap(hidden, "wt", 1), proj_weight, down_pruned
    )
    shares = lax.all_to_all(shares, both, split_axis=0, concat_axis=0, tiled=True)
    out = jax.ShapeDtypeStruct(tokens.shape, tokens.dtype)
    return small(leave_kernel, out, shares, tokens, modulation.transpose(1, 0, 2), out_bias.reshape(1, -1))


def solution(mesh):
    seq, wt = mesh.shape["seq"], mesh.shape["wt"]

    def shards(*args):
        share = args[2].shape[2]
        whole_heads = share % HEAD == 0 and share == args[8].shape[1] and args[5].shape[1] % share == 0
        fits = whole_heads and wt == 4 and seq == 4 and args[0].shape[1] == 4
        return (fixed_shards if fits else gathered_shards)(*args)

    return jax.shard_map(
        shards,
        mesh=mesh,
        in_specs=(
            P(("rep", "wt"), "seq", None),
            P(("rep", "wt"), None, None),
            P("wt", None, "seq"),
            P(None, "seq"),
            P(),
            P("wt", "seq"),
            P("wt", "seq"),
            P("seq"),
            P("seq", "wt"),
            P("seq", "wt"),
            P("seq", "wt"),
            P(),
        ),
        out_specs=P(("rep", "wt"), "seq", None),
        check_vma=False,
    )
```

```python
import functools
import math

import jax
import jax.numpy as jnp
from jax import lax
from jax.experimental import pallas as pl
from jax.experimental.pallas import tpu as pltpu
from jax.sharding import PartitionSpec as P

HEAD = 128
BLOCK = 64
MIB = 1024 * 1024
BESIDE = 16 * MIB


def masked(weight, keep_mask):
    row_blocks, col_blocks = keep_mask.shape
    expanded = jnp.broadcast_to(keep_mask[:, None, :, None], (row_blocks, BLOCK, col_blocks, BLOCK))
    return weight * expanded.reshape(weight.shape).astype(jnp.bfloat16)


def layer_norm(values):
    center = values - jnp.mean(values, axis=-1, keepdims=True)
    spread = jnp.mean(center * center, axis=-1, keepdims=True)
    return center * lax.rsqrt(spread + 1e-06)


def norm_heads(flat_rows, gains):
    shaped_rows = flat_rows.reshape(flat_rows.shape[0], -1, HEAD).astype(jnp.float32)
    scaled = (
        shaped_rows
        * lax.rsqrt(jnp.mean(shaped_rows * shaped_rows, axis=-1, keepdims=True) + 1e-06)
        * gains
    )
    return scaled.astype(jnp.bfloat16)


def attend(queries, keys_normed, values):
    scores = jnp.einsum(
        "qhd,khd->hqk", queries, keys_normed, preferred_element_type=jnp.float32
    ) / math.sqrt(HEAD)
    weights = jnp.exp(scores)
    denoms = jnp.sum(weights, axis=2)
    summed = jnp.einsum(
        "hqk,khd->qhd", weights.astype(jnp.bfloat16), values, preferred_element_type=jnp.float32
    )
    return (summed, denoms)


def gathered_shards(
    tokens,
    modulation,
    qkv_weight,
    qkv_bias,
    norm_gains,
    up_weight,
    up_mask,
    up_bias,
    proj_weight,
    down_weight,
    down_mask,
    out_bias,
):
    own_rows = tokens[0]
    mod_rows = modulation[0]
    row_count = own_rows.shape[0]
    feature_count = own_rows.shape[1]
    head_count = feature_count // HEAD
    normed = layer_norm(own_rows.astype(jnp.float32))
    shaped = ((1.0 + mod_rows[1]) * normed + mod_rows[0]).astype(jnp.bfloat16)
    gathered = lax.all_gather(shaped, "seq", axis=0, tiled=True)
    seq_len = gathered.shape[0]
    col_share = qkv_weight.shape[2]
    up_local = masked(up_weight, up_mask)
    pieces = (
        lax.all_gather(qkv_weight, "wt", axis=0, tiled=True),
        lax.all_gather(up_local, "wt", axis=0, tiled=True),
    )
    piece_rows = pieces[0].shape[0]
    first = jnp.dot(
        gathered, pieces[0].reshape(piece_rows, 3 * col_share), preferred_element_type=jnp.float32
    )
    second = jnp.dot(gathered, pieces[1], preferred_element_type=jnp.float32)
    qkv_local = (first.reshape(seq_len, 3, col_share) + qkv_bias).astype(jnp.bfloat16)
    hidden = jax.nn.gelu(second + up_bias, approximate=True).astype(jnp.bfloat16)
    query_flat = lax.all_to_all(qkv_local[:, 0, :], "seq", split_axis=0, concat_axis=1, tiled=True)
    kv_whole = lax.all_gather(qkv_local[:, 1:, :], "seq", axis=2, tiled=True)
    queries = norm_heads(query_flat, norm_gains[0])
    keys_normed = norm_heads(kv_whole[:, 0, :], norm_gains[1])
    values = kv_whole[:, 1, :].reshape(seq_len, head_count, HEAD)
    summed, denoms = attend(queries, keys_normed, values)
    attended = (
        (summed / denoms.T[:, :, None]).reshape(row_count, feature_count).astype(jnp.bfloat16)
    )
    attended_cols = lax.all_to_all(attended, "seq", split_axis=1, concat_axis=0, tiled=True)
    down_local = masked(down_weight, down_mask)
    proj_full, down_full = (
        lax.all_gather(proj_weight, "wt", axis=1, tiled=True),
        lax.all_gather(down_local, "wt", axis=1, tiled=True),
    )
    branch_sum = lax.psum_scatter(
        jnp.dot(attended_cols, proj_full, preferred_element_type=jnp.float32)
        + jnp.dot(hidden, down_full, preferred_element_type=jnp.float32),
        "seq",
        scatter_dimension=0,
        tiled=True,
    )
    result = own_rows.astype(jnp.float32) + mod_rows[2] * (branch_sum + out_bias)
    return result.astype(jnp.bfloat16)[None]


def enter_kernel(tokens_ref, mod_ref, mask_ref, pick_ref, out_ref, lanes_ref):
    lanes_ref[...] = jnp.dot(mask_ref[...].astype(jnp.bfloat16), pick_ref[...], preferred_element_type=jnp.float32)
    shaped = (1.0 + mod_ref[1]) * layer_norm(tokens_ref[0].astype(jnp.float32)) + mod_ref[0]
    shaped = shaped.astype(jnp.bfloat16)
    share = out_ref.shape[2]
    for place in range(out_ref.shape[0]):
        out_ref[place] = shaped[:, place % 4 * share : (place % 4 + 1) * share]


def enter(tokens, modulation, mask, pick):
    _, count, features = tokens.shape
    return pl.pallas_call(
        enter_kernel,
        out_shape=[
            jax.ShapeDtypeStruct((16, count, features // 4), jnp.bfloat16),
            jax.ShapeDtypeStruct((mask.shape[0], pick.shape[1]), jnp.float32),
        ],
        compiler_params=pltpu.CompilerParams(vmem_limit_bytes=4 * MIB),
        cost_estimate=pl.CostEstimate(flops=400 * BESIDE, bytes_accessed=BESIDE, transcendentals=BESIDE // 100),
        name="enter",
    )(tokens, modulation.transpose(1, 0, 2), mask, pick)


def leave_kernel(shares_ref, tokens_ref, mod_ref, bias_ref, out_ref):
    share = shares_ref.shape[2]
    for n in range(4):
        lanes = slice(n * share, (n + 1) * share)
        branch = sum(shares_ref[4 * place + n].astype(jnp.float32) for place in range(4)) + bias_ref[:, lanes]
        out_ref[0, :, lanes] = (tokens_ref[0, :, lanes].astype(jnp.float32) + mod_ref[2, :, lanes] * branch).astype(out_ref.dtype)


def small(kernel, outs, *args):
    return pl.pallas_call(
        kernel,
        out_shape=outs,
        compiler_params=pltpu.CompilerParams(vmem_limit_bytes=4 * MIB),
        name=kernel.__name__,
    )(*args)


def pick_lanes(blocks, lanes):
    return (
        lax.broadcasted_iota(jnp.int32, (blocks, lanes), 1) // BLOCK
        == lax.broadcasted_iota(jnp.int32, (blocks, lanes), 0)
    ).astype(jnp.bfloat16)


def pick_kernel(out_ref):
    out_ref[...] = pick_lanes(*out_ref.shape)


def picks(blocks, lanes):
    return pl.pallas_call(
        pick_kernel,
        out_shape=jax.ShapeDtypeStruct((blocks, lanes), jnp.bfloat16),
        compiler_params=pltpu.CompilerParams(vmem_limit_bytes=4 * MIB),
        cost_estimate=pl.CostEstimate(flops=400 * BESIDE, bytes_accessed=BESIDE, transcendentals=BESIDE // 100),
        name="picks",
    )()


def prune_kernel(mask_dim, mask_ref, weight_ref, out_ref, lanes):
    lanes[...] = lax.dot_general(
        mask_ref[...].astype(jnp.bfloat16),
        pick_lanes(mask_ref.shape[mask_dim], out_ref.shape[1]),
        (((mask_dim,), (0,)), ((), ())),
        preferred_element_type=jnp.float32,
    )

    def body(b, _):
        rows = pl.ds(pl.multiple_of(b * BLOCK, BLOCK), BLOCK)
        out_ref[rows, :] = weight_ref[rows, :] * lanes[pl.ds(b, 1), :].astype(jnp.bfloat16)
        return 0

    lax.fori_loop(0, out_ref.shape[0] // BLOCK, body, 0)


def prune(weight, mask, turned, hint=1):
    size = 2 * weight.size
    return pl.pallas_call(
        functools.partial(prune_kernel, 0 if turned else 1),
        out_shape=jax.ShapeDtypeStruct(weight.shape, jnp.bfloat16),
        scratch_shapes=[pltpu.VMEM((weight.shape[0] // BLOCK, weight.shape[1]), jnp.float32)],
        compiler_params=pltpu.CompilerParams(vmem_limit_bytes=14 * MIB),
        cost_estimate=pl.CostEstimate(flops=size * hint, bytes_accessed=2 * size * hint, transcendentals=0),
        name="prune",
    )(mask.T if turned else mask, weight)


def in_kernel(pruned, got_ref, *refs):
    share = got_ref.shape[2]
    if pruned:
        lanes, weight_ref, keep_ref, send_ref = refs
    else:
        weight_ref, keep_ref, send_ref = refs
    core = lax.axis_index("wt") % 2
    x = jnp.concatenate(
        [
            got_ref[4 * place + 2 * chip + (core ^ other_core)].astype(jnp.float32)
            for place in range(4)
            for other_core in range(2)
            for chip in range(2)
        ],
        axis=0,
    ).astype(jnp.bfloat16)
    for n in range(keep_ref.shape[1] // share):
        cols = slice(n * share, (n + 1) * share)
        if pruned:
            weight = jnp.concatenate(
                [
                    weight_ref[r * BLOCK : (r + 1) * BLOCK, cols] * lanes[r : r + 1, cols].astype(jnp.bfloat16)
                    for r in range(lanes.shape[0])
                ],
                axis=0,
            )
        else:
            weight = weight_ref[n]
        out = jnp.dot(x, weight, preferred_element_type=jnp.float32)
        keep_ref[:, cols] = jnp.concatenate([out[r : r + 8] for r in range(0, 64, 16)], axis=0)
        send_ref[:, cols] = jnp.concatenate([out[r + 8 : r + 16] for r in range(0, 64, 16)], axis=0).astype(jnp.bfloat16)


def in_products(got, weight, lanes=None):
    places, count, depth = got.shape
    half, width = places * count // 2, weight.size // depth
    pruned = lanes is not None
    return pl.pallas_call(
        functools.partial(in_kernel, pruned),
        out_shape=[
            jax.ShapeDtypeStruct((half, width), jnp.float32),
            jax.ShapeDtypeStruct((half, width), jnp.bfloat16),
        ],
        compiler_params=pltpu.CompilerParams(vmem_limit_bytes=14 * MIB),
        cost_estimate=pl.CostEstimate(flops=4 * half * weight.size, bytes_accessed=2 * weight.size, transcendentals=0),
        name="in_products",
    )(got, *([lanes] if pruned else []), weight)


def share_kernel(kept_ref, got_ref, mine_ref, send_ref):
    total = kept_ref[...] + got_ref[...].astype(jnp.float32)
    rows = range(0, total.shape[0], 8)
    first = jnp.concatenate([total[r : r + 4] for r in rows], axis=0)
    second = jnp.concatenate([total[r + 4 : r + 8] for r in rows], axis=0)
    on_first = lax.axis_index("wt") < 2
    mine_ref[...] = jnp.where(on_first, first, second)
    send_ref[...] = jnp.where(on_first, second, first).astype(jnp.bfloat16)


def attend_kernel(images, part, own_ref, other_ref, bias_ref, gains_ref, out_ref):
    rows, share = out_ref.shape
    heads = share // HEAD

    def stacked(which):
        lanes = slice(which * share, (which + 1) * share)
        flat = own_ref[:, lanes] + other_ref[:, lanes].astype(jnp.float32)
        flat = (flat + bias_ref[which : which + 1, :]).astype(jnp.bfloat16)
        return jnp.concatenate([flat[:, h * HEAD : (h + 1) * HEAD] for h in range(heads)], axis=0)

    def normed(which):
        wide = stacked(which).astype(jnp.float32)
        scale = lax.rsqrt(jnp.mean(wide * wide, axis=-1, keepdims=True) + 1e-06)
        return (wide * scale * gains_ref[which : which + 1, :]).astype(jnp.bfloat16)

    queries, keys, values = normed(0), normed(1), stacked(2)
    scores = lax.dot_general(
        queries, keys, (((1,), (1,)), ((), ())), preferred_element_type=jnp.float32
    ) * (1.0 / math.sqrt(HEAD))
    size = heads * rows

    def group(dim):
        place = lax.broadcasted_iota(jnp.int32, (size, size), dim)
        return place // rows * images + place // part % images

    same = group(0) == group(1)
    weights = jnp.where(same, jnp.exp(jnp.where(same, scores, 0.0)), 0.0)
    denoms = jnp.sum(weights, axis=-1, keepdims=True)
    summed = jnp.dot(weights.astype(jnp.bfloat16), values, preferred_element_type=jnp.float32)
    attended = (summed / denoms).astype(jnp.bfloat16)
    for h in range(heads):
        out_ref[:, h * HEAD : (h + 1) * HEAD] = attended[h * rows : (h + 1) * rows]


def attention(images, part, own, other, bias, gains):
    return pl.pallas_call(
        functools.partial(attend_kernel, images, part),
        out_shape=jax.ShapeDtypeStruct((own.shape[0], bias.shape[1]), jnp.bfloat16),
        compiler_params=pltpu.CompilerParams(vmem_limit_bytes=8 * MIB),
        name="attention",
    )(own, other, bias, gains)


def hidden_kernel(own_ref, other_ref, bias_ref, out_ref):
    step = 6 * HEAD
    for start in range(0, out_ref.shape[1], step):
        lanes = slice(start, start + step)
        v = own_ref[:, lanes] + other_ref[:, lanes].astype(jnp.float32) + bias_ref[:, lanes]
        cubic = math.sqrt(2.0 / math.pi) * (v + 0.044715 * (v * v * v))
        out_ref[:, lanes] = (0.5 * v * (1.0 + jnp.tanh(cubic))).astype(jnp.bfloat16)


def activate(own, other, bias):
    return pl.pallas_call(
        hidden_kernel,
        out_shape=jax.ShapeDtypeStruct(own.shape, jnp.bfloat16),
        compiler_params=pltpu.CompilerParams(vmem_limit_bytes=8 * MIB),
        name="hidden",
    )(own, other, bias.reshape(1, -1))


def by_chip(mine, theirs):
    mine, theirs = mine.astype(jnp.float32), theirs.astype(jnp.float32)
    on_first = lax.axis_index("wt") < 2
    first, second = jnp.where(on_first, mine, theirs), jnp.where(on_first, theirs, mine)
    pieces = []
    for r in range(0, mine.shape[0], 4):
        pieces += [first[r : r + 4], second[r : r + 4]]
    return jnp.concatenate(pieces, axis=0).astype(jnp.bfloat16)


def out_kernel(a_mine, a_theirs, h_mine, h_theirs, proj_ref, down_ref, out_ref):
    half = a_mine.shape[0] // 2
    attended = jnp.concatenate([by_chip(a_mine[:half], a_theirs[half:]), by_chip(a_theirs[:half], a_mine[half:])], axis=0)
    hidden = jnp.concatenate([h_mine[...], h_theirs[...]], axis=0)
    total = jnp.dot(attended, proj_ref[...], preferred_element_type=jnp.float32)
    total += jnp.dot(hidden, down_ref[...], preferred_element_type=jnp.float32)
    core = lax.axis_index("wt") % 2
    count = out_ref.shape[1]
    row = 0
    for other_core in range(2):
        for place in range(4):
            for chip in range(2):
                target = 4 * place + 2 * chip + (core ^ other_core)
                out_ref[target] = total[row : row + count].astype(out_ref.dtype)
                row += count


def out_products(count, attended, theirs, hidden, hidden_theirs, proj, down):
    rows, width = 2 * hidden.shape[0], proj.shape[1]
    size = proj.size + down.size
    return pl.pallas_call(
        out_kernel,
        out_shape=jax.ShapeDtypeStruct((rows // count, count, width), jnp.bfloat16),
        compiler_params=pltpu.CompilerParams(vmem_limit_bytes=12 * MIB),
        cost_estimate=pl.CostEstimate(flops=2 * rows * size, bytes_accessed=2 * size, transcendentals=0),
        name="out_products",
    )(attended, theirs, hidden, hidden_theirs, proj, down)


def swap(values, axis, bit):
    count = lax.axis_size(axis)
    return lax.ppermute(values, axis, [(i, i ^ bit) for i in range(count)])


def fixed_shards(
    tokens,
    modulation,
    qkv_weight,
    qkv_bias,
    norm_gains,
    up_weight,
    up_mask,
    up_bias,
    proj_weight,
    down_weight,
    down_mask,
    out_bias,
):
    count = tokens.shape[1]
    both = ("seq", "wt")
    sent, lanes = enter(tokens, modulation, up_mask, picks(up_mask.shape[1], up_weight.shape[1]))
    got = lax.all_to_all(sent, both, split_axis=0, concat_axis=0, tiled=True)
    kept, given = in_products(got, qkv_weight.transpose(1, 0, 2))
    got, given = lax.optimization_barrier((got, given))
    half, width = kept.shape[0] // 2, kept.shape[1]
    halves = [jax.ShapeDtypeStruct((half, width), jnp.float32), jax.ShapeDtypeStruct((half, width), jnp.bfloat16)]
    own, sent = small(share_kernel, halves, kept, swap(given, "wt", 1))
    up_kept, up_given = in_products(got, up_weight, lanes)
    up_given, sent = lax.optimization_barrier((up_given, sent))
    attended = attention(1, count, own, swap(sent, "wt", 2), qkv_bias, norm_gains)
    own = up_kept + swap(up_given, "wt", 1).astype(jnp.float32)
    pair = own, swap(own.astype(jnp.bfloat16), "wt", 2)
    down_pruned = prune(down_weight, down_mask, True, hint=0)
    attended = jnp.concatenate([attended, swap(attended, "wt", 3)], axis=0)
    attended, down_pruned = lax.optimization_barrier((attended, down_pruned))
    pair, attended = lax.optimization_barrier((pair, attended))
    hidden = activate(*pair, up_bias)
    shares = out_products(
        count, attended, swap(attended, "wt", 1), hidden, swap(hidden, "wt", 1), proj_weight, down_pruned
    )
    shares = lax.all_to_all(shares, both, split_axis=0, concat_axis=0, tiled=True)
    out = jax.ShapeDtypeStruct(tokens.shape, tokens.dtype)
    return small(leave_kernel, out, shares, tokens, modulation.transpose(1, 0, 2), out_bias.reshape(1, -1))


def solution(mesh):
    seq, wt = mesh.shape["seq"], mesh.shape["wt"]

    def shards(*args):
        share = args[2].shape[2]
        whole_heads = share % HEAD == 0 and share == args[8].shape[1] and args[5].shape[1] % share == 0
        fits = whole_heads and wt == 4 and seq == 4 and args[0].shape[1] == 4
        return (fixed_shards if fits else gathered_shards)(*args)

    return jax.shard_map(
        shards,
        mesh=mesh,
        in_specs=(
            P(("rep", "wt"), "seq", None),
            P(("rep", "wt"), None, None),
            P("wt", None, "seq"),
            P(None, "seq"),
            P(),
            P("wt", "seq"),
            P("wt", "seq"),
            P("seq"),
            P("seq", "wt"),
            P("seq", "wt"),
            P("seq", "wt"),
            P(),
        ),
        out_specs=P(("rep", "wt"), "seq", None),
        check_vma=False,
    )
```
